32 devices in a mesh: replica: 8 (over y, x, core), fsdp: 4 (over z).
Axes of the slice: x: 2, y: 2, z: 4, core: 2. Of those that a mesh axis runs over, the one named last changes fastest.
Arguments:
- latents: bfloat16 [65536, 64], P(('replica', 'fsdp')), may hold values from -6 to 6
- target: bfloat16 [65536, 64], P(('replica', 'fsdp')), may hold values from -6 to 6
- timesteps: int32 [128], P(('replica', 'fsdp')), may hold values from 0 to 999
- patch_weight: float32 [8, 64, 5120], P('replica', None, 'fsdp'), may hold values from -0.75 to 0.75
- head_weight: float32 [8, 64, 5120], P('replica', None, 'fsdp'), may hold values from -0.078125 to 0.078125
- modulation: float32 [8, 2, 5120], P('replica', None, 'fsdp'), may hold values from -3 to 3
- time_weight: float32 [8, 256, 5120], P('replica', None, 'fsdp'), may hold values from -0.375 to 0.375
- anchor: float32 [5120, 5120], P('fsdp', 'replica'), may hold values from -6 to 6
- momentum: float32 [5120, 5120], P('fsdp', 'replica'), may hold values from -4 to 4
- frag_start: bfloat16 [5120, 5120], P('fsdp'), may hold values from -4.1 to 4.1, as said below
- frag_current: bfloat16 [8, 5120, 5120], P('replica', 'fsdp'), may hold values from -10.1 to 10.1, as said below
Outputs:
- patch_new: float32 [8, 64, 5120], P('replica', None, 'fsdp')
- head_new: float32 [8, 64, 5120], P('replica', None, 'fsdp')
- modulation_new: float32 [8, 2, 5120], P('replica', None, 'fsdp')
- time_new: float32 [8, 256, 5120], P('replica', None, 'fsdp')
- new_anchor: float32 [5120, 5120], P('fsdp', 'replica')
- new_momentum: float32 [5120, 5120], P('fsdp', 'replica')
- new_params: bfloat16 [5120, 5120], P('fsdp')
The draws below stay inside these ranges and needn't reach their ends.
Inputs may be any that keep to these rules, and one draw needn't show every extreme that they name: `frag_start`: every entry is at least 0.02 in magnitude. `frag_current`: every entry is at least 0.02 in magnitude.
All inputs are finite; a program needn't handle non-finite values.
Results may differ from the reference program's by a relative error of at most 0.028.
Values may be sent and summed in bfloat16 or wider, within the bound.
A program may use at most 192 MiB of HBM per device.

```python
import math
import jax
import jax.numpy as jnp
from jax import lax

D = 5120
FREQ_DIM = 256
PATCH_DIM = 64
QBLOCK = 128
SAMPLE_TOKENS = 512
SAMPLES = 128
TOKENS = 65536
REPLICAS = 8
N_REPLICA = 8


def lift_magnitude(values):
    return jnp.where(values >= 0.0, values + 0.02, values - 0.02)


def rough_noise(key, shape):
    normal_part = jnp.clip(jax.random.normal(key, shape, jnp.float32), -4.0, 4.0)
    return normal_part


def fragment_base(key):
    return lift_magnitude(rough_noise(key, (D, D))).astype(jnp.bfloat16)


def draw_frag_start(key, part):
    return fragment_base(key)


def draw_frag_current(key, part):
    low_scale = 0.25
    start = fragment_base(key).astype(jnp.float32)
    key = jax.random.fold_in(key, 5)
    noise_key, column_key, row_key = jax.random.split(key, 3)
    drift_noise = rough_noise(noise_key, (REPLICAS, D, D))
    column_scale = jnp.exp(jax.random.uniform(column_key, (REPLICAS, 1, D), jnp.float32, math.log(low_scale), 0.0))
    row_scale = jnp.exp(jax.random.uniform(row_key, (1, D, 1), jnp.float32, math.log(0.5), math.log(1.5)))
    drift = drift_noise * column_scale * row_scale
    return lift_magnitude(start[None] - drift).astype(jnp.bfloat16)


def touch_ends(array, stream_key, low, high):
    longest = array.shape.index(max(array.shape))
    spots = []
    for shift in (0, 1):
        where = [jax.random.randint(jax.random.fold_in(stream_key, axis), (), 0, length) for axis, length in enumerate(array.shape)]
        where[longest] = (where[longest] + shift) % array.shape[longest]
        spots.append(tuple(where))
    return array.at[spots[0]].set(low).at[spots[1]].set(high)


def shard_levels(key, dims, pieces, smallest, largest):
    gain, own = 1.0, jax.random.fold_in(key, 6)
    for axis_at, blocks in pieces:
        heights = jnp.exp(jax.random.uniform(jax.random.fold_in(own, axis_at), (blocks,), jnp.float32, smallest / len(pieces), largest / len(pieces)))
        gain = gain * jnp.repeat(heights, dims[axis_at] // blocks).reshape([-1 if axis == axis_at else 1 for axis in range(len(dims))])
    return gain


def gaussian(stream_key, dims, scale, bound, cuts=(), kind=jnp.bfloat16):
    entries = jax.random.normal(stream_key, dims, jnp.float32) * scale
    if len(cuts) > 0:
        entries = shard_levels(stream_key, dims, cuts, -0.22, 0.18) * entries
    return jnp.clip(entries, min=-bound, max=bound).astype(kind)


def setup_inputs(seed: int = 0) -> dict:
    arg_keys = jax.random.split(jax.random.key(seed), 12)
    return {
        "latents": gaussian(arg_keys[0], (TOKENS, PATCH_DIM), 1.0, 6.0, ((0, 32),)),
        "target": gaussian(arg_keys[1], (TOKENS, PATCH_DIM), 1.0, 6.0, ((0, 32),)),
        "timesteps": touch_ends(jax.random.randint(arg_keys[2], (SAMPLES,), 0, 1000), jax.random.fold_in(arg_keys[2], 1), 0, 999).astype(jnp.int32),
        "patch_weight": gaussian(arg_keys[3], (REPLICAS, PATCH_DIM, D), PATCH_DIM ** -0.5, 0.75, ((0, 8), (2, 4)), jnp.float32),
        "head_weight": gaussian(arg_keys[4], (REPLICAS, PATCH_DIM, D), D ** -0.5, 0.078125, ((0, 8), (2, 4)), jnp.float32),
        "modulation": gaussian(arg_keys[5], (REPLICAS, 2, D), 0.3, 3.0, ((0, 8), (2, 4)), jnp.float32),
        "time_weight": gaussian(arg_keys[6], (REPLICAS, FREQ_DIM, D), FREQ_DIM ** -0.5, 0.375, ((0, 8), (2, 4)), jnp.float32),
        "anchor": gaussian(arg_keys[7], (D, D), 1.0, 6.0, ((0, 4), (1, 8)), jnp.float32),
        "momentum": gaussian(arg_keys[8], (D, D), 0.3, 4.0, ((0, 4), (1, 8)), jnp.float32),
        "frag_start": draw_frag_start(jax.random.fold_in(arg_keys[11], 71), 0),
        "frag_current": draw_frag_current(jax.random.fold_in(arg_keys[11], 71), 0),
    }


epsilon = 1e-06
inner_rate = 0.5
outer_rate = 0.7
momentum_decay = 0.9

def sinusoid(time_steps):
    index = jnp.arange(FREQ_DIM // 2, dtype=jnp.float32)
    frequency = jnp.exp(-math.log(10000.0) * index / (FREQ_DIM // 2))
    angles = time_steps.astype(jnp.float32)[:, None] * frequency[None, :]
    return jnp.concatenate([jnp.cos(angles), jnp.sin(angles)], axis=1)

def silu_slope(pre_act):
    sigmoid_val = jax.nn.sigmoid(pre_act)
    return sigmoid_val * (1.0 + pre_act * (1.0 - sigmoid_val))

def quantize(blocks, scale_bf):
    scale_f = scale_bf.astype(jnp.float32)[:, None, :]
    seven_abs = 7.0 * jnp.abs(blocks)
    levels = jnp.zeros_like(blocks)
    for rung_index in range(7):
        levels = levels + (seven_abs >= (rung_index + 0.5) * scale_f).astype(jnp.float32)
    return (jnp.sign(blocks) * levels).astype(jnp.bfloat16)

def make_visitor(patch_bf, head_bf, mod_bf, tok_count):

    def visit_block(totals, inputs):
        latent_blk, target_blk, embed_row = inputs
        hidden = jnp.dot(latent_blk, patch_bf, preferred_element_type=jnp.float32)
        center = hidden - lax.optimization_barrier(jnp.mean(hidden, axis=1, keepdims=True))
        inv_std = lax.rsqrt(lax.optimization_barrier(jnp.mean(center * center, axis=1, keepdims=True)) + epsilon)
        normed = center * inv_std
        gain_row = 1.0 + mod_bf[1].astype(jnp.float32) + embed_row
        modulated = (normed * gain_row + mod_bf[0].astype(jnp.float32) + embed_row).astype(jnp.bfloat16)
        output = lax.dot_general(modulated, head_bf, (((1,), (1,)), ((), ())), preferred_element_type=jnp.float32)
        grad_out = (2.0 * (output - target_blk.astype(jnp.float32)) / tok_count).astype(jnp.bfloat16)
        grad_head = lax.dot_general(grad_out, modulated, (((0,), (0,)), ((), ())), preferred_element_type=jnp.float32)
        grad_mixed = jnp.dot(grad_out, head_bf, preferred_element_type=jnp.float32)
        grad_shift = lax.optimization_barrier(jnp.sum(grad_mixed, axis=0))
        grad_scale = lax.optimization_barrier(jnp.sum(grad_mixed * normed, axis=0))
        grad_normed = grad_mixed * gain_row
        grad_hidden = ((grad_normed - lax.optimization_barrier(jnp.mean(grad_normed, axis=1, keepdims=True)) - normed * lax.optimization_barrier(jnp.mean(grad_normed * normed, axis=1, keepdims=True))) * inv_std).astype(jnp.bfloat16)
        grad_patch = lax.dot_general(latent_blk, grad_hidden, (((0,), (0,)), ((), ())), preferred_element_type=jnp.float32)
        new_totals = (totals[0] + grad_patch, totals[1] + grad_head, totals[2] + jnp.stack([grad_shift, grad_scale]))
        return (new_totals, grad_shift + grad_scale)
    return visit_block

def inner_replica(latent_r, target_r, steps_r, patch_r, head_r, mod_r, time_r):
    patch_bf = patch_r.astype(jnp.bfloat16)
    head_bf = head_r.astype(jnp.bfloat16)
    mod_bf = mod_r.astype(jnp.bfloat16)
    time_bf = time_r.astype(jnp.bfloat16)
    sines = sinusoid(steps_r).astype(jnp.bfloat16)
    pre_act = jnp.dot(sines, time_bf, preferred_element_type=jnp.float32)
    embed = jax.nn.silu(pre_act)
    sample_count = steps_r.shape[0]
    tok_count = latent_r.shape[0] * 1.0
    latent_blocks = latent_r.reshape(sample_count, SAMPLE_TOKENS, PATCH_DIM)
    target_blocks = target_r.reshape(sample_count, SAMPLE_TOKENS, PATCH_DIM)
    start_totals = (jnp.zeros((PATCH_DIM, D), jnp.float32), jnp.zeros((PATCH_DIM, D), jnp.float32), jnp.zeros((2, D), jnp.float32))
    totals, grad_embed = lax.scan(make_visitor(patch_bf, head_bf, mod_bf, tok_count), start_totals, (latent_blocks, target_blocks, embed))
    grad_pre = (grad_embed * silu_slope(pre_act)).astype(jnp.bfloat16)
    grad_time = lax.dot_general(sines, grad_pre, (((0,), (0,)), ((), ())), preferred_element_type=jnp.float32)
    return (patch_r - inner_rate * totals[0], head_r - inner_rate * totals[1], mod_r - inner_rate * totals[2], time_r - inner_rate * grad_time)

def per_replica(packed):
    return inner_replica(*packed)

def reference(latents, target, timesteps, patch_weight, head_weight, modulation, time_weight, anchor, momentum, frag_start, frag_current):
    packed = (latents.reshape(N_REPLICA, -1, PATCH_DIM), target.reshape(N_REPLICA, -1, PATCH_DIM), timesteps.reshape(N_REPLICA, -1), patch_weight, head_weight, modulation, time_weight)
    patch_new, head_new, modulation_new, time_new = lax.map(per_replica, packed)
    start_f = frag_start.astype(jnp.float32)

    def add_replica(total, current):
        delta = start_f - current.astype(jnp.float32)
        blocks = delta.reshape(D // QBLOCK, QBLOCK, D)
        scale = (lax.optimization_barrier(jnp.max(jnp.abs(blocks), axis=1)) + epsilon).astype(jnp.bfloat16)
        code = quantize(blocks, scale)
        term = (code.astype(jnp.float32) * scale.astype(jnp.float32)[:, None, :] / 7.0).reshape(D, D)
        return (total + term, None)
    total, unused = lax.scan(add_replica, jnp.zeros((D, D), jnp.float32), frag_current)
    average = total / N_REPLICA
    new_momentum = momentum_decay * momentum + average
    new_anchor = anchor - outer_rate * (average + momentum_decay * new_momentum)
    new_params = new_anchor.astype(jnp.bfloat16)
    return (patch_new, head_new, modulation_new, time_new, new_anchor, new_momentum, new_params)
```

```python
import math

import jax
import jax.numpy as jnp
from jax import lax
from jax.experimental import pallas as pl
from jax.experimental.pallas import tpu as pltpu
from jax.sharding import PartitionSpec as P

FREQ_DIM = 256
PATCH_DIM = 64
QBLOCK = 128
SAMPLE_TOKENS = 512

epsilon = 1e-06
inner_rate = 0.5
outer_rate = 0.7
momentum_decay = 0.9

MESH = pl.DeviceIdType.MESH
EXACT = lax.Precision.HIGHEST
TIE_UP = 1.0 + 2.0**-22


def sinusoid(time_steps):
    index = jnp.arange(FREQ_DIM // 2, dtype=jnp.float32)
    frequency = jnp.exp(-math.log(10000.0) * index / (FREQ_DIM // 2))
    angles = time_steps.astype(jnp.float32)[:, None] * frequency[None, :]
    return jnp.concatenate([jnp.cos(angles), jnp.sin(angles)], axis=1)


def silu_slope(pre_act):
    sigmoid_val = jax.nn.sigmoid(pre_act)
    return sigmoid_val * (1.0 + pre_act * (1.0 - sigmoid_val))


def fdot(spec, a, b):
    return jnp.einsum(spec, a, b, precision=EXACT, preferred_element_type=jnp.float32)


def nearest(values):
    return lax.round(values, lax.RoundingMethod.TO_NEAREST_EVEN)


def flip(index, bit):
    return index + bit - 2 * bit * lax.rem(index // bit, 2)


def fragment_kernel(
    blocks,
    cols,
    start_hbm,
    cur_hbm,
    anchor_hbm,
    mom_hbm,
    anchor_out,
    mom_out,
    params_out,
    start_v,
    cur_v,
    terms,
    got1,
    got2,
    got3,
    anchor_v,
    mom_v,
    own,
    load_sem,
    state_sem,
    store_sem,
    s_send,
    s_recv,
    g_send,
    g_recv,
    own_sem,
):
    me = lax.axis_index("replica")
    core = lax.rem(me, 2)
    rows = QBLOCK
    sibling = flip(me, 1)

    def load(i, slot):
        span = pl.ds(pl.multiple_of(i * rows, rows), rows)
        return (
            pltpu.make_async_copy(start_hbm.at[span, :], start_v.at[slot], load_sem.at[slot, 0]),
            pltpu.make_async_copy(cur_hbm.at[span, :], cur_v.at[slot], load_sem.at[slot, 1]),
        )

    def bits(i):
        first = 2 + 2 * lax.rem(i, 2)
        return first, 6 - first

    def send(src, dst, send_sem, recv_sem, to):
        return pltpu.make_async_remote_copy(
            src_ref=src,
            dst_ref=dst,
            send_sem=send_sem,
            recv_sem=recv_sem,
            device_id={"replica": to},
            device_id_type=MESH,
        )

    def pair_at(who, fixed, other, k):
        chip = who // 2
        f, o = fixed // 2, other // 2
        return f * lax.rem(chip // f, 2) + o * k

    def step1(i):
        return send(
            terms.at[i, 1 - core], got1.at[i], s_send.at[0, i], s_recv.at[0, i], sibling
        )

    def step2(i):
        first, second = bits(i)
        to = flip(me, first)
        return [
            send(
                terms.at[i, core, pair_at(to, first, second, k)],
                got2.at[i, k],
                s_send.at[1 + k, i],
                s_recv.at[1 + k, i],
                to,
            )
            for k in range(2)
        ]

    def step3(i):
        first, second = bits(i)
        to = flip(me, second)
        return send(
            terms.at[i, core, to // 2], got3.at[i], s_send.at[3, i], s_recv.at[3, i], to
        )

    def place(i, who):
        span = pl.ds(pl.multiple_of(i * rows, rows), rows)
        return params_out.at[span, pl.ds(pl.multiple_of(who * cols, 128), cols)]

    def back3(i):
        first, second = bits(i)
        return send(
            own.at[i], place(i, me), g_send.at[0, i], g_recv.at[0, i], flip(me, second)
        )

    def back2(i):
        first, second = bits(i)
        to = flip(me, first)
        near = flip(me, second)
        return [
            send(own.at[i], place(i, me), g_send.at[1, i], g_recv.at[1, i], to),
            send(place(i, near), place(i, near), g_send.at[2, i], g_recv.at[2, i], to),
        ]

    def back1(i):
        first, second = bits(i)
        whos = (flip(me, second), flip(me, first), flip(flip(me, first), second))
        sends = [send(own.at[i], place(i, me), g_send.at[3, i], g_recv.at[3, i], sibling)]
        for n, who in enumerate(whos):
            sends.append(
                send(place(i, who), place(i, who), g_send.at[4 + n, i], g_recv.at[4 + n, i], sibling)
            )
        return sends

    def keep(i):
        return pltpu.make_async_copy(own.at[i], place(i, me), own_sem.at[i])

    state_loads = (
        pltpu.make_async_copy(anchor_hbm, anchor_v, state_sem.at[0]),
        pltpu.make_async_copy(mom_hbm, mom_v, state_sem.at[1]),
    )
    for copy in load(0, 0):
        copy.start()
    for copy in state_loads:
        copy.start()

    barrier = pltpu.get_barrier_semaphore()
    for bit in (1, 2, 4):
        pl.semaphore_signal(
            barrier, inc=1, device_id={"replica": flip(me, bit)}, device_id_type=MESH
        )
    pl.semaphore_wait(barrier, 3)

    def quantize(i):
        slot = lax.rem(i, 2)
        for copy in load(i, slot):
            copy.wait()

        @pl.when(i + 1 < blocks)
        def _():
            for copy in load(i + 1, 1 - slot):
                copy.start()

        for who in range(8):
            for part in range(cols // 128):
                lanes = pl.ds(who * cols + part * 128, 128)
                delta = start_v[slot, :, lanes].astype(jnp.float32) - cur_v[
                    slot, :, lanes
                ].astype(jnp.float32)
                top = jnp.max(jnp.abs(delta), axis=0, keepdims=True)
                scale = (top + epsilon).astype(jnp.bfloat16).astype(jnp.float32)
                level = nearest(delta * (7.0 * TIE_UP / scale))
                level = jnp.clip(level, -7.0, 7.0)
                terms[i, who % 2, who // 2, :, pl.ds(part * 128, 128)] = (
                    level * (scale / 7.0)
                ).astype(jnp.bfloat16)
        step1(i).start()

    def fold1(i):
        step1(i).wait()
        for k in range(4):
            terms[i, core, k] = (
                terms[i, core, k].astype(jnp.float32) + got1[i, k].astype(jnp.float32)
            ).astype(jnp.bfloat16)
        for copy in step2(i):
            copy.start()

    def fold2(i):
        for copy in step2(i):
            copy.wait()
        first, second = bits(i)
        for k in range(2):
            at = pair_at(me, first, second, k)
            terms[i, core, at] = (
                terms[i, core, at].astype(jnp.float32) + got2[i, k].astype(jnp.float32)
            ).astype(jnp.bfloat16)
        step3(i).start()

    def update(i):
        step3(i).wait()

        @pl.when(i == 0)
        def _():
            for copy in state_loads:
                copy.wait()

        span = pl.ds(pl.multiple_of(i * rows, rows), rows)
        average = (
            terms[i, core, me // 2].astype(jnp.float32) + got3[i].astype(jnp.float32)
        ) / 8.0
        new_momentum = momentum_decay * mom_v[span, :] + average
        new_anchor = anchor_v[span, :] - outer_rate * (average + momentum_decay * new_momentum)
        mom_v[span, :] = new_momentum
        anchor_v[span, :] = new_anchor
        own[i] = new_anchor.astype(jnp.bfloat16)
        back3(i).start()
        keep(i).start()
        pltpu.make_async_copy(anchor_v.at[span, :], anchor_out.at[span, :], store_sem.at[0, i]).start()
        pltpu.make_async_copy(mom_v.at[span, :], mom_out.at[span, :], store_sem.at[1, i]).start()

    def spread2(i):
        back3(i).wait()
        for copy in back2(i):
            copy.start()

    def spread1(i):
        for copy in back2(i):
            copy.wait()
        for copy in back1(i):
            copy.start()

    stages = ((0, quantize), (1, fold1), (3, fold2), (5, update), (7, spread2), (9, spread1))

    def step(i, carry):
        for lag, stage in stages:

            @pl.when(jnp.logical_and(i >= lag, i < blocks + lag))
            def _(stage=stage, lag=lag):
                stage(i - lag)

        return carry

    lax.fori_loop(0, blocks + stages[-1][0], step, 0)

    def finish(i, carry):
        span = pl.ds(pl.multiple_of(i * rows, rows), rows)
        for copy in back1(i):
            copy.wait()
        keep(i).wait()
        pltpu.make_async_copy(anchor_v.at[span, :], anchor_out.at[span, :], store_sem.at[0, i]).wait()
        pltpu.make_async_copy(mom_v.at[span, :], mom_out.at[span, :], store_sem.at[1, i]).wait()
        return carry

    lax.fori_loop(0, blocks, finish, 0)


def fragment_by_kernel(anchor, momentum, frag_start, frag_current):
    rows, width = frag_start.shape
    blocks, cols = rows // QBLOCK, anchor.shape[1]
    bf16, f32 = jnp.bfloat16, jnp.float32
    dma = pltpu.SemaphoreType.DMA
    return pl.pallas_call(
        lambda *refs: fragment_kernel(blocks, cols, *refs),
        out_shape=(
            jax.ShapeDtypeStruct((rows, cols), f32),
            jax.ShapeDtypeStruct((rows, cols), f32),
            jax.ShapeDtypeStruct((rows, width), bf16),
        ),
        in_specs=[pl.BlockSpec(memory_space=pl.ANY)] * 4,
        out_specs=(pl.BlockSpec(memory_space=pl.ANY),) * 3,
        scratch_shapes=[
            pltpu.VMEM((2, QBLOCK, width), bf16),
            pltpu.VMEM((2, QBLOCK, width), bf16),
            pltpu.VMEM((blocks, 2, 4, QBLOCK, cols), bf16),
            pltpu.VMEM((blocks, 4, QBLOCK, cols), bf16),
            pltpu.VMEM((blocks, 2, QBLOCK, cols), bf16),
            pltpu.VMEM((blocks, QBLOCK, cols), bf16),
            pltpu.VMEM((rows, cols), f32),
            pltpu.VMEM((rows, cols), f32),
            pltpu.VMEM((blocks, QBLOCK, cols), bf16),
            dma((2, 2)),
            dma((2,)),
            dma((2, blocks)),
            dma((4, blocks)),
            dma((4, blocks)),
            dma((7, blocks)),
            dma((7, blocks)),
            dma((blocks,)),
        ],
        compiler_params=pltpu.CompilerParams(
            collective_id=0, has_side_effects=True, vmem_limit_bytes=56 * 1024 * 1024
        ),
        cost_estimate=pl.CostEstimate(
            flops=20 * rows * width, bytes_accessed=8 * rows * width, transcendentals=0
        ),
        name="fragment_sync",
    )(frag_start, frag_current, anchor, momentum)


def fragment_by_collectives(anchor, momentum, frag_start, frag_current):
    replica_count = lax.axis_size("replica")
    delta = frag_start.astype(jnp.float32) - frag_current.astype(jnp.float32)
    rows, width = delta.shape
    blocks = delta.reshape(rows // QBLOCK, QBLOCK, width)
    top = jnp.max(jnp.abs(blocks), axis=1, keepdims=True)
    scale = lax.reduce_precision(top + epsilon, 8, 7)
    level = jnp.clip(nearest(blocks * (7.0 * TIE_UP / scale)), -7.0, 7.0)
    terms = (level * (scale / 7.0)).astype(jnp.bfloat16).reshape(rows, width)
    total = lax.psum_scatter(terms, "replica", scatter_dimension=1, tiled=True)
    average = total.astype(jnp.float32) / replica_count
    new_momentum = momentum_decay * momentum + average
    new_anchor = anchor - outer_rate * (average + momentum_decay * new_momentum)
    new_params = lax.all_gather(new_anchor.astype(jnp.bfloat16), "replica", axis=1, tiled=True)
    return new_anchor, new_momentum, new_params


def inner_step(latents, target, timesteps, patch_weight, head_weight, modulation, time_weight):
    fsdp = lax.axis_size("fsdp")
    here = timesteps.shape[0]
    samples = here * fsdp
    width = patch_weight.shape[2]
    full = width * fsdp
    tok_count = latents.shape[0] * fsdp * 1.0
    f32 = jnp.float32

    sines = sinusoid(lax.all_gather(timesteps, "fsdp", tiled=True)).astype(jnp.bfloat16)
    wp = patch_weight[0].astype(jnp.bfloat16).astype(f32)
    wh = head_weight[0].astype(jnp.bfloat16).astype(f32)
    wm = modulation[0].astype(jnp.bfloat16).astype(f32)
    pre_act = jnp.dot(sines, time_weight[0].astype(jnp.bfloat16), preferred_element_type=f32)
    embed = jax.nn.silu(pre_act)
    gain = 1.0 + wm[1] + embed
    shift = wm[0] + embed

    mean_here = jnp.mean(wp, axis=1)
    wp_here = wp - mean_here[:, None]
    gained = wh[None] * gain[:, None, :]
    gram = fdot("if,kf->ik", wp_here, wp_here)
    mix = fdot("sjf,if->sij", gained, wp_here)
    gained_sum = jnp.sum(gained, axis=2)
    offset = fdot("sf,jf->sj", shift, wh)

    def split(a):
        return a.reshape(fsdp, -1, PATCH_DIM)

    def copies(a):
        return jnp.broadcast_to(a.reshape(1, -1, PATCH_DIM), (fsdp, a.size // PATCH_DIM, PATCH_DIM))

    sent = jnp.concatenate(
        [split(mix), split(gained_sum), split(offset), copies(gram), copies(mean_here)], axis=1
    )
    got = lax.all_to_all(sent, "fsdp", 0, 0)
    a, b = here * PATCH_DIM, here * PATCH_DIM + here
    mean_of = got[:, -1]
    mean = jnp.mean(mean_of, axis=0)
    off_mean = mean_of - mean
    gained_sum_of = got[:, a:b]
    mix = jnp.sum(got[:, :a], axis=0).reshape(here, PATCH_DIM, PATCH_DIM) + jnp.sum(
        off_mean[:, None, :, None] * gained_sum_of[:, :, None, :], axis=0
    )
    gained_mean = jnp.sum(gained_sum_of, axis=0) / full
    offset = jnp.sum(got[:, b : b + here], axis=0)
    gram = jnp.sum(got[:, b + here : -1], axis=0) + width * jnp.sum(
        off_mean[:, :, None] * off_mean[:, None, :], axis=0
    )
    gram = gram / full

    lat = latents.astype(f32)
    var = jnp.sum(fdot("ti,ik->tk", lat, gram) * lat, axis=1, keepdims=True)
    inv_std = lax.rsqrt(jnp.maximum(var, 0.0) + epsilon)
    lat = (lat * inv_std).reshape(here, SAMPLE_TOKENS, PATCH_DIM)
    centred = fdot("sti,sij->stj", lat, mix)
    wanted = target.reshape(here, SAMPLE_TOKENS, PATCH_DIM).astype(f32)
    output = centred + offset[:, None, :]
    grad_out = (2.0 * (output - wanted) / tok_count).astype(jnp.bfloat16).astype(f32)
    first = jnp.sum(grad_out * gained_mean[:, None, :], axis=2, keepdims=True)
    second = jnp.sum(grad_out * centred, axis=2, keepdims=True) / full
    cross = fdot("sti,stj->sij", lat, grad_out)
    square = fdot("sti,stk->ik", lat * second, lat)
    lean = jnp.sum(lat * first, axis=(0, 1))
    out_sum = jnp.sum(grad_out, axis=1)

    sent = jnp.concatenate(
        [cross.reshape(-1, PATCH_DIM), out_sum, square, lean[None]], axis=0
    )
    got = lax.all_gather(sent, "fsdp")
    cross = got[:, :a].reshape(samples, PATCH_DIM, PATCH_DIM)
    out_sum = got[:, a:b].reshape(samples, PATCH_DIM)
    square = jnp.sum(got[:, b:-1], axis=0)
    lean = jnp.sum(got[:, -1], axis=0)

    centre = wp - mean[:, None]
    turned = fdot("sij,if->sjf", cross, centre)
    grad_head = jnp.sum(turned * gain[:, None, :], axis=0) + fdot("sj,sf->jf", out_sum, shift)
    grad_scale = jnp.sum(turned * wh[None], axis=1)
    grad_shift = fdot("sj,jf->sf", out_sum, wh)
    grad_patch = (
        fdot("sij,sjf->if", cross, gained)
        - lean[:, None]
        - fdot("ik,kf->if", square, centre)
    )
    grad_mod = jnp.stack([jnp.sum(grad_shift, axis=0), jnp.sum(grad_scale, axis=0)])
    grad_pre = ((grad_shift + grad_scale) * silu_slope(pre_act)).astype(jnp.bfloat16)
    grad_time = lax.dot_general(
        sines, grad_pre, (((0,), (0,)), ((), ())), preferred_element_type=f32
    )
    return (
        patch_weight - inner_rate * grad_patch[None],
        head_weight - inner_rate * grad_head[None],
        modulation - inner_rate * grad_mod[None],
        time_weight - inner_rate * grad_time[None],
    )


def per_device(
    latents,
    target,
    timesteps,
    patch_weight,
    head_weight,
    modulation,
    time_weight,
    anchor,
    momentum,
    frag_start,
    frag_current,
):
    inner = inner_step(
        latents, target, timesteps, patch_weight, head_weight, modulation, time_weight
    )
    if lax.axis_size("replica") == 8 and anchor.shape[1] % 128 == 0:
        fragment = fragment_by_kernel
    else:
        fragment = fragment_by_collectives
    return inner + tuple(fragment(anchor, momentum, frag_start, frag_current[0]))


def solution(mesh):
    in_specs = (
        P(("replica", "fsdp"), None),
        P(("replica", "fsdp"), None),
        P(("replica", "fsdp")),
        P("replica", None, "fsdp"),
        P("replica", None, "fsdp"),
        P("replica", None, "fsdp"),
        P("replica", None, "fsdp"),
        P("fsdp", "replica"),
        P("fsdp", "replica"),
        P("fsdp", None),
        P("replica", "fsdp", None),
    )
    out_specs = (
        P("replica", None, "fsdp"),
        P("replica", None, "fsdp"),
        P("replica", None, "fsdp"),
        P("replica", None, "fsdp"),
        P("fsdp", "replica"),
        P("fsdp", "replica"),
        P("fsdp", None),
    )
    return jax.shard_map(
        per_device, mesh=mesh, in_specs=in_specs, out_specs=out_specs, check_vma=False
    )
```

```python
import math

import jax
import jax.numpy as jnp
from jax import lax
from jax.experimental import pallas as pl
from jax.experimental.pallas import tpu as pltpu
from jax.sharding import PartitionSpec as P

FREQ_DIM = 256
PATCH_DIM = 64
QBLOCK = 128
SAMPLE_TOKENS = 512

epsilon = 1e-06
inner_rate = 0.5
outer_rate = 0.7
momentum_decay = 0.9

MESH = pl.DeviceIdType.MESH
EXACT = lax.Precision.HIGHEST
TIE_UP = 1.0 + 2.0**-22


def sinusoid(time_steps):
    index = jnp.arange(FREQ_DIM // 2, dtype=jnp.float32)
    frequency = jnp.exp(-math.log(10000.0) * index / (FREQ_DIM // 2))
    angles = time_steps.astype(jnp.float32)[:, None] * frequency[None, :]
    return jnp.concatenate([jnp.cos(angles), jnp.sin(angles)], axis=1)


def silu_slope(pre_act):
    sigmoid_val = jax.nn.sigmoid(pre_act)
    return sigmoid_val * (1.0 + pre_act * (1.0 - sigmoid_val))


def fdot(spec, a, b):
    return jnp.einsum(spec, a, b, precision=EXACT, preferred_element_type=jnp.float32)


def nearest(values):
    return lax.round(values, lax.RoundingMethod.TO_NEAREST_EVEN)


def flip(index, bit):
    return index + bit - 2 * bit * lax.rem(index // bit, 2)


def window_kernel(
    blocks,
    cols,
    peers,
    here,
    start_hbm,
    cur_hbm,
    anchor_hbm,
    mom_hbm,
    lat_in,
    target_in,
    sines_in,
    patch_in,
    head_in,
    mod_in,
    time_in,
    patch_out,
    head_out,
    mod_out,
    time_out,
    anchor_out,
    mom_out,
    params_out,
    start_v,
    cur_v,
    terms,
    got1,
    got2,
    got3,
    anchor_v,
    mom_v,
    own,
    load_sem,
    state_sem,
    store_sem,
    s_send,
    s_recv,
    g_send,
    g_recv,
    own_sem,
    sines_all,
    pre,
    gain,
    shift,
    out1,
    in1,
    out2,
    in2,
    total1,
    extra1,
    wide,
    scale_rows,
    sum_rows,
    z_send,
    z_recv,
):
    f32, bf16 = jnp.float32, jnp.bfloat16
    z = lax.axis_index("fsdp")
    width = patch_in.shape[1]
    full = width * peers
    group = here * PATCH_DIM
    tok_count = here * SAMPLE_TOKENS * peers * 1.0
    me = lax.axis_index("replica")
    core = lax.rem(me, 2)
    rows = QBLOCK
    sibling = flip(me, 1)

    def load(i, slot):
        span = pl.ds(pl.multiple_of(i * rows, rows), rows)
        return (
            pltpu.make_async_copy(start_hbm.at[span, :], start_v.at[slot], load_sem.at[slot, 0]),
            pltpu.make_async_copy(cur_hbm.at[span, :], cur_v.at[slot], load_sem.at[slot, 1]),
        )

    def bits(i):
        first = 2 + 2 * lax.rem(i, 2)
        return first, 6 - first

    def send(src, dst, send_sem, recv_sem, to):
        return pltpu.make_async_remote_copy(
            src_ref=src,
            dst_ref=dst,
            send_sem=send_sem,
            recv_sem=recv_sem,
            device_id={"replica": to},
            device_id_type=MESH,
        )

    def pair_at(who, fixed, other, k):
        chip = who // 2
        f, o = fixed // 2, other // 2
        return f * lax.rem(chip // f, 2) + o * k

    def step1(i):
        return send(
            terms.at[i, 1 - core], got1.at[i], s_send.at[0, i], s_recv.at[0, i], sibling
        )

    def step2(i):
        first, second = bits(i)
        to = flip(me, first)
        return [
            send(
                terms.at[i, core, pair_at(to, first, second, k)],
                got2.at[i, k],
                s_send.at[1 + k, i],
                s_recv.at[1 + k, i],
                to,
            )
            for k in range(2)
        ]

    def step3(i):
        first, second = bits(i)
        to = flip(me, second)
        return send(
            terms.at[i, core, to // 2], got3.at[i], s_send.at[3, i], s_recv.at[3, i], to
        )

    def place(i, who):
        span = pl.ds(pl.multiple_of(i * rows, rows), rows)
        return params_out.at[span, pl.ds(pl.multiple_of(who * cols, 128), cols)]

    def back3(i):
        first, second = bits(i)
        return send(
            own.at[i], place(i, me), g_send.at[0, i], g_recv.at[0, i], flip(me, second)
        )

    def back2(i):
        first, second = bits(i)
        to = flip(me, first)
        near = flip(me, second)
        return [
            send(own.at[i], place(i, me), g_send.at[1, i], g_recv.at[1, i], to),
            send(place(i, near), place(i, near), g_send.at[2, i], g_recv.at[2, i], to),
        ]

    def back1(i):
        first, second = bits(i)
        whos = (flip(me, second), flip(me, first), flip(flip(me, first), second))
        sends = [send(own.at[i], place(i, me), g_send.at[3, i], g_recv.at[3, i], sibling)]
        for n, who in enumerate(whos):
            sends.append(
                send(place(i, who), place(i, who), g_send.at[4 + n, i], g_recv.at[4 + n, i], sibling)
            )
        return sends

    def keep(i):
        return pltpu.make_async_copy(own.at[i], place(i, me), own_sem.at[i])

    state_loads = (
        pltpu.make_async_copy(anchor_hbm, anchor_v, state_sem.at[0]),
        pltpu.make_async_copy(mom_hbm, mom_v, state_sem.at[1]),
    )
    for copy in load(0, 0):
        copy.start()
    for copy in state_loads:
        copy.start()

    barrier = pltpu.get_barrier_semaphore()
    for bit in (1, 2, 4):
        pl.semaphore_signal(
            barrier, inc=1, device_id={"replica": flip(me, bit)}, device_id_type=MESH
        )
    for k in range(1, peers):
        pl.semaphore_signal(
            barrier, inc=1, device_id={"fsdp": lax.rem(z + k, peers)}, device_id_type=MESH
        )
    pl.semaphore_wait(barrier, 3 + peers - 1)


    def zsend(src, dst, what, k):
        return pltpu.make_async_remote_copy(
            src_ref=src,
            dst_ref=dst,
            send_sem=z_send.at[what, k - 1],
            recv_sem=z_recv.at[what, k - 1],
            device_id={"fsdp": lax.rem(z + k, peers)},
            device_id_type=MESH,
        )

    def sines_copy(k):
        return zsend(sines_in, sines_all.at[z], 0, k)

    def first_copy(k):
        return zsend(out1.at[k - 1], in1.at[z], 1, k)

    def second_copy(k):
        return zsend(out2, in2.at[z], 2, k)

    def halves(values):
        high = values.astype(bf16)
        return high, (values - high.astype(f32)).astype(bf16)

    def dot(a, b, dims):
        return lax.dot_general(a, b, (dims, ((), ())), preferred_element_type=f32)

    def dot2(a, b, dims):
        high, low = halves(b)
        return dot(a, high, dims) + dot(a, low, dims)

    def dot3(a, b, dims):
        a_high, a_low = halves(a)
        b_high, b_low = halves(b)
        return dot(a_high, b_high, dims) + dot(a_high, b_low, dims) + dot(a_low, b_high, dims)

    nt, nn, tn = ((1,), (1,)), ((1,), (0,)), ((0,), (0,))

    sines_all[z] = sines_in[...]
    for k in range(1, peers):
        sines_copy(k).start()

    def rounded(ref):
        return ref[...].astype(bf16).astype(f32)

    def inner_open():
        for k in range(1, peers):
            sines_copy(k).wait()
        sines = sines_all[...].reshape(peers * 8, FREQ_DIM).astype(bf16)
        pre_act = dot(sines, time_in[...].astype(bf16), nn)
        pre[...] = pre_act
        embed = pre_act * jax.nn.sigmoid(pre_act)
        mod = rounded(mod_in)
        gain[...] = 1.0 + mod[1:2] + embed
        shift[...] = mod[0:1] + embed

    def inner_first(k):
        to = lax.rem(z + k, peers)
        rows8 = pl.ds(pl.multiple_of(to * 8, 8), 8)
        raw = patch_in[...].astype(bf16)
        wp = raw.astype(f32)
        wp = wp - jnp.sum(wp, axis=1, keepdims=True) / width
        wh = rounded(head_in)
        gains = gain[rows8, :]
        parts = [wh * gains[q : q + 1] for q in range(here)]
        gained = jnp.concatenate(parts, axis=0)
        mix = dot3(gained, wp, nt)
        sums = jnp.sum(gained, axis=1, keepdims=True)
        shift_high, shift_low = halves(shift[rows8, :])
        head_bf = wh.astype(bf16)
        offset = dot(shift_high, head_bf, nt) + dot(shift_low, head_bf, nt)
        mean_rows = dot(jnp.ones((8, width), bf16), raw, nt) / width

        def put(ref):
            ref[pl.ds(0, group), 0:64] = mix
            ref[pl.ds(0, group), 64:128] = jnp.broadcast_to(sums, (group, 64))
            ref[pl.ds(group, 64), 0:64] = dot3(wp, wp, nt)
            ref[pl.ds(group, 64), 64:128] = jnp.zeros((64, 64), f32)
            ref[pl.ds(group + 64, 8), 0:64] = offset
            ref[pl.ds(group + 64, 8), 64:128] = jnp.zeros((8, 64), f32)
            ref[pl.ds(group + 72, 8), 0:64] = mean_rows
            ref[pl.ds(group + 72, 8), 64:128] = jnp.zeros((8, 64), f32)

        if k == 0:
            put(in1.at[z])
        else:
            put(out1.at[k - 1])
            first_copy(k).start()

    def inner_gather():
        for k in range(1, peers):
            first_copy(k).wait()
        means = [in1[d, pl.ds(group + 72, 8), 0:64] for d in range(peers)]
        mean = sum(means[1:], means[0]) / peers
        offs = [m - mean for m in means]
        mix = jnp.zeros((group, 64), f32)
        sums = jnp.zeros((group, 64), f32)
        gram = jnp.zeros((64, 64), f32)
        offset = jnp.zeros((8, 64), f32)
        for d in range(peers):
            wide_sum = in1[d, pl.ds(0, group), 64:128]
            mix = mix + in1[d, pl.ds(0, group), 0:64] + wide_sum * offs[d][0:1]
            sums = sums + wide_sum
            gram = gram + in1[d, pl.ds(group, 64), 0:64]
            gram = gram + (width / 8.0) * dot3(offs[d], offs[d], tn)
            offset = offset + in1[d, pl.ds(group + 64, 8), 0:64]
        total1[pl.ds(0, group), 0:64] = mix
        total1[pl.ds(0, group), 64:128] = sums / full
        total1[pl.ds(group, 64), 0:64] = gram / full
        total1[pl.ds(group, 64), 64:128] = dot2(jnp.ones((64, 8), bf16), mean, nn).T / 8.0
        extra1[...] = offset
        out2[...] = jnp.zeros_like(out2)

    def inner_sample(q):
        span = pl.ds(q * SAMPLE_TOKENS, SAMPLE_TOKENS)
        at = pl.ds(q * PATCH_DIM, PATCH_DIM)
        lat_bf = lat_in[span, :]
        lat = lat_bf.astype(f32)
        gram = total1[pl.ds(group, 64), 0:64]
        var = jnp.sum(dot2(lat_bf, gram, nn) * lat, axis=1, keepdims=True)
        inv_std = lax.rsqrt(jnp.maximum(var, 0.0) + epsilon)
        centred = dot2(lat_bf, total1[at, 0:64], nt) * inv_std
        output = centred + extra1[q : q + 1, :]
        grad_out = (2.0 * (output - target_in[span, :].astype(f32)) / tok_count).astype(bf16)
        grad_f = grad_out.astype(f32)
        first = dot2(grad_out, total1[at, 64:128], nn)
        second = jnp.sum(grad_f * centred, axis=1, keepdims=True) / full
        lat = lat * inv_std
        wide[:, 0:64] = lat * second
        wide[:, 64:128] = first
        out2[at, 0:64] = dot2(grad_out, lat, tn)
        out2[pl.ds(group, 64), :] += dot3(lat, wide[...], tn)
        out2[pl.ds(group + 64 + q, 1), 0:64] = jnp.sum(grad_f, axis=0, keepdims=True)

    def inner_second():
        in2[z] = out2[...]
        for k in range(1, peers):
            second_copy(k).start()

    def inner_close():
        for k in range(1, peers):
            second_copy(k).wait()
        rest = in2[0, pl.ds(group, 64), :]
        for d in range(1, peers):
            rest = rest + in2[d, pl.ds(group, 64), :]
        centre = rounded(patch_in) - total1[pl.ds(group, 64), 64:65]
        patch_out[...] = patch_in[...] + inner_rate * (
            rest[:, 64:65] + dot3(rest[:, 0:64], centre, nn)
        )
        for d in range(peers):
            sum_rows[pl.ds(8 * d, 8), :] = in2[d, pl.ds(group + 64, 8), 0:64]
        head_out[...] = head_in[...] - inner_rate * dot3(sum_rows[...], shift[...], tn)
        scale_rows[...] = jnp.zeros_like(scale_rows)

    def inner_source(d):
        centre = rounded(patch_in) - total1[pl.ds(group, 64), 64:65]
        wh = rounded(head_in)
        cross = in2[d, pl.ds(0, group), 0:64]
        turned = dot3(cross, centre, nn)
        parts = []
        head_sum = jnp.zeros_like(wh)
        for q in range(here):
            row = gain[8 * d + q : 8 * d + q + 1, :]
            piece = turned[q * 64 : q * 64 + 64]
            head_sum = head_sum + piece * row
            scale_rows[8 * d + q : 8 * d + q + 1, :] = jnp.sum(piece * wh, axis=0, keepdims=True)
            parts.append(wh * row)
        head_out[...] -= inner_rate * head_sum
        patch_out[...] -= inner_rate * dot3(cross, jnp.concatenate(parts, axis=0), tn)

    def inner_end():
        grad_scale = scale_rows[...]
        high, low = halves(sum_rows[...])
        head_bf = head_in[...].astype(bf16)
        grad_shift = dot(high, head_bf, nn) + dot(low, head_bf, nn)
        mod_out[0:1, :] = mod_in[0:1, :] - inner_rate * jnp.sum(grad_shift, axis=0, keepdims=True)
        mod_out[1:2, :] = mod_in[1:2, :] - inner_rate * jnp.sum(grad_scale, axis=0, keepdims=True)
        sines = sines_all[...].reshape(peers * 8, FREQ_DIM).astype(bf16)
        grad_pre = ((grad_shift + grad_scale) * silu_slope(pre[...])).astype(bf16)
        time_out[...] = time_in[...] - inner_rate * dot(sines, grad_pre, tn)

    def quantize(i):
        slot = lax.rem(i, 2)
        for copy in load(i, slot):
            copy.wait()

        @pl.when(i + 1 < blocks)
        def _():
            for copy in load(i + 1, 1 - slot):
                copy.start()

        for who in range(8):
            for part in range(cols // 128):
                lanes = pl.ds(who * cols + part * 128, 128)
                delta = start_v[slot, :, lanes].astype(jnp.float32) - cur_v[
                    slot, :, lanes
                ].astype(jnp.float32)
                top = jnp.max(jnp.abs(delta), axis=0, keepdims=True)
                scale = (top + epsilon).astype(jnp.bfloat16).astype(jnp.float32)
                level = nearest(delta * (7.0 * TIE_UP / scale))
                level = jnp.clip(level, -7.0, 7.0)
                terms[i, who % 2, who // 2, :, pl.ds(part * 128, 128)] = (
                    level * (scale / 7.0)
                ).astype(jnp.bfloat16)
        step1(i).start()

    def fold1(i):
        step1(i).wait()
        for k in range(4):
            terms[i, core, k] = (
                terms[i, core, k].astype(jnp.float32) + got1[i, k].astype(jnp.float32)
            ).astype(jnp.bfloat16)
        for copy in step2(i):
            copy.start()

    def fold2(i):
        for copy in step2(i):
            copy.wait()
        first, second = bits(i)
        for k in range(2):
            at = pair_at(me, first, second, k)
            terms[i, core, at] = (
                terms[i, core, at].astype(jnp.float32) + got2[i, k].astype(jnp.float32)
            ).astype(jnp.bfloat16)
        step3(i).start()

    def update(i):
        step3(i).wait()

        @pl.when(i == 0)
        def _():
            for copy in state_loads:
                copy.wait()

        span = pl.ds(pl.multiple_of(i * rows, rows), rows)
        average = (
            terms[i, core, me // 2].astype(jnp.float32) + got3[i].astype(jnp.float32)
        ) / 8.0
        new_momentum = momentum_decay * mom_v[span, :] + average
        new_anchor = anchor_v[span, :] - outer_rate * (average + momentum_decay * new_momentum)
        mom_v[span, :] = new_momentum
        anchor_v[span, :] = new_anchor
        own[i] = new_anchor.astype(jnp.bfloat16)
        back3(i).start()
        keep(i).start()
        pltpu.make_async_copy(anchor_v.at[span, :], anchor_out.at[span, :], store_sem.at[0, i]).start()
        pltpu.make_async_copy(mom_v.at[span, :], mom_out.at[span, :], store_sem.at[1, i]).start()

    def spread2(i):
        back3(i).wait()
        for copy in back2(i):
            copy.start()

    def spread1(i):
        for copy in back2(i):
            copy.wait()
        for copy in back1(i):
            copy.start()

    stages = ((0, quantize), (1, fold1), (3, fold2), (5, update), (7, spread2), (9, spread1))

    parts = [(2, inner_open)]
    parts += [(3 + k, lambda k=k: inner_first(peers - 1 - k)) for k in range(peers)]
    at = 5 + peers
    parts += [(at, inner_gather)]
    parts += [(at + q, lambda q=q: inner_sample(q)) for q in range(here)]
    at += here
    parts += [(at - 1, inner_second), (at + 1, inner_close)]
    parts += [(at + 1 + d, lambda d=d: inner_source(d)) for d in range(peers)]
    parts += [(at + 1 + peers, inner_end)]

    def step(i, carry):
        for when, part in parts:

            @pl.when(i == when)
            def _(part=part):
                part()

        for lag, stage in stages:

            @pl.when(jnp.logical_and(i >= lag, i < blocks + lag))
            def _(stage=stage, lag=lag):
                stage(i - lag)

        return carry

    lax.fori_loop(0, max(blocks + stages[-1][0], parts[-1][0] + 1), step, 0)

    def finish(i, carry):
        span = pl.ds(pl.multiple_of(i * rows, rows), rows)
        for copy in back1(i):
            copy.wait()
        keep(i).wait()
        pltpu.make_async_copy(anchor_v.at[span, :], anchor_out.at[span, :], store_sem.at[0, i]).wait()
        pltpu.make_async_copy(mom_v.at[span, :], mom_out.at[span, :], store_sem.at[1, i]).wait()
        return carry

    lax.fori_loop(0, blocks, finish, 0)


def window_by_kernel(
    latents,
    target,
    timesteps,
    patch_weight,
    head_weight,
    modulation,
    time_weight,
    anchor,
    momentum,
    frag_start,
    frag_current,
):
    rows, span = frag_start.shape
    blocks, cols = rows // QBLOCK, anchor.shape[1]
    peers, here = lax.axis_size("fsdp"), timesteps.shape[0]
    width = patch_weight.shape[2]
    group = here * PATCH_DIM
    bf16, f32 = jnp.bfloat16, jnp.float32
    dma = pltpu.SemaphoreType.DMA
    sines = lax.reduce_precision(sinusoid(timesteps), 8, 7)
    sines = jnp.pad(sines, ((0, 8 - here), (0, 0)))
    params = (patch_weight[0], head_weight[0], modulation[0], time_weight[0])
    out = pl.pallas_call(
        lambda *refs: window_kernel(blocks, cols, peers, here, *refs),
        out_shape=tuple(jax.ShapeDtypeStruct(p.shape, f32) for p in params)
        + (
            jax.ShapeDtypeStruct((rows, cols), f32),
            jax.ShapeDtypeStruct((rows, cols), f32),
            jax.ShapeDtypeStruct((rows, span), bf16),
        ),
        in_specs=[pl.BlockSpec(memory_space=pl.ANY)] * 4
        + [pl.BlockSpec(memory_space=pltpu.VMEM)] * 7,
        out_specs=(pl.BlockSpec(memory_space=pltpu.VMEM),) * 4
        + (pl.BlockSpec(memory_space=pl.ANY),) * 3,
        scratch_shapes=[
            pltpu.VMEM((2, QBLOCK, span), bf16),
            pltpu.VMEM((2, QBLOCK, span), bf16),
            pltpu.VMEM((blocks, 2, 4, QBLOCK, cols), bf16),
            pltpu.VMEM((blocks, 4, QBLOCK, cols), bf16),
            pltpu.VMEM((blocks, 2, QBLOCK, cols), bf16),
            pltpu.VMEM((blocks, QBLOCK, cols), bf16),
            pltpu.VMEM((rows, cols), f32),
            pltpu.VMEM((rows, cols), f32),
            pltpu.VMEM((blocks, QBLOCK, cols), bf16),
            dma((2, 2)),
            dma((2,)),
            dma((2, blocks)),
            dma((4, blocks)),
            dma((4, blocks)),
            dma((7, blocks)),
            dma((7, blocks)),
            dma((blocks,)),
            pltpu.VMEM((peers, 8, FREQ_DIM), f32),
            pltpu.VMEM((peers * 8, width), f32),
            pltpu.VMEM((peers * 8, width), f32),
            pltpu.VMEM((peers * 8, width), f32),
            pltpu.VMEM((peers - 1, group + 80, 128), f32),
            pltpu.VMEM((peers, group + 80, 128), f32),
            pltpu.VMEM((group + 72, 128), f32),
            pltpu.VMEM((peers, group + 72, 128), f32),
            pltpu.VMEM((group + 64, 128), f32),
            pltpu.VMEM((8, 64), f32),
            pltpu.VMEM((SAMPLE_TOKENS, 128), f32),
            pltpu.VMEM((peers * 8, width), f32),
            pltpu.VMEM((peers * 8, 64), f32),
            dma((3, peers - 1)),
            dma((3, peers - 1)),
        ],
        compiler_params=pltpu.CompilerParams(
            collective_id=0, has_side_effects=True, vmem_limit_bytes=60 * 1024 * 1024
        ),
        cost_estimate=pl.CostEstimate(
            flops=20 * rows * span, bytes_accessed=8 * rows * span, transcendentals=0
        ),
        name="window",
    )(frag_start, frag_current, anchor, momentum, latents, target, sines, *params)
    return tuple(o[None] for o in out[:4]) + tuple(out[4:])


def fragment_by_collectives(anchor, momentum, frag_start, frag_current):
    replica_count = lax.axis_size("replica")
    delta = frag_start.astype(jnp.float32) - frag_current.astype(jnp.float32)
    rows, width = delta.shape
    blocks = delta.reshape(rows // QBLOCK, QBLOCK, width)
    top = jnp.max(jnp.abs(blocks), axis=1, keepdims=True)
    scale = lax.reduce_precision(top + epsilon, 8, 7)
    level = jnp.clip(nearest(blocks * (7.0 * TIE_UP / scale)), -7.0, 7.0)
    terms = (level * (scale / 7.0)).astype(jnp.bfloat16).reshape(rows, width)
    total = lax.psum_scatter(terms, "replica", scatter_dimension=1, tiled=True)
    average = total.astype(jnp.float32) / replica_count
    new_momentum = momentum_decay * momentum + average
    new_anchor = anchor - outer_rate * (average + momentum_decay * new_momentum)
    new_params = lax.all_gather(new_anchor.astype(jnp.bfloat16), "replica", axis=1, tiled=True)
    return new_anchor, new_momentum, new_params


def inner_step(latents, target, timesteps, patch_weight, head_weight, modulation, time_weight):
    fsdp = lax.axis_size("fsdp")
    here = timesteps.shape[0]
    samples = here * fsdp
    width = patch_weight.shape[2]
    full = width * fsdp
    tok_count = latents.shape[0] * fsdp * 1.0
    f32 = jnp.float32

    sines = sinusoid(lax.all_gather(timesteps, "fsdp", tiled=True)).astype(jnp.bfloat16)
    wp = patch_weight[0].astype(jnp.bfloat16).astype(f32)
    wh = head_weight[0].astype(jnp.bfloat16).astype(f32)
    wm = modulation[0].astype(jnp.bfloat16).astype(f32)
    pre_act = jnp.dot(sines, time_weight[0].astype(jnp.bfloat16), preferred_element_type=f32)
    embed = jax.nn.silu(pre_act)
    gain = 1.0 + wm[1] + embed
    shift = wm[0] + embed

    mean_here = jnp.mean(wp, axis=1)
    wp_here = wp - mean_here[:, None]
    gained = wh[None] * gain[:, None, :]
    gram = fdot("if,kf->ik", wp_here, wp_here)
    mix = fdot("sjf,if->sij", gained, wp_here)
    gained_sum = jnp.sum(gained, axis=2)
    offset = fdot("sf,jf->sj", shift, wh)

    def split(a):
        return a.reshape(fsdp, -1, PATCH_DIM)

    def copies(a):
        return jnp.broadcast_to(a.reshape(1, -1, PATCH_DIM), (fsdp, a.size // PATCH_DIM, PATCH_DIM))

    sent = jnp.concatenate(
        [split(mix), split(gained_sum), split(offset), copies(gram), copies(mean_here)], axis=1
    )
    got = lax.all_to_all(sent, "fsdp", 0, 0)
    a, b = here * PATCH_DIM, here * PATCH_DIM + here
    mean_of = got[:, -1]
    mean = jnp.mean(mean_of, axis=0)
    off_mean = mean_of - mean
    gained_sum_of = got[:, a:b]
    mix = jnp.sum(got[:, :a], axis=0).reshape(here, PATCH_DIM, PATCH_DIM) + jnp.sum(
        off_mean[:, None, :, None] * gained_sum_of[:, :, None, :], axis=0
    )
    gained_mean = jnp.sum(gained_sum_of, axis=0) / full
    offset = jnp.sum(got[:, b : b + here], axis=0)
    gram = jnp.sum(got[:, b + here : -1], axis=0) + width * jnp.sum(
        off_mean[:, :, None] * off_mean[:, None, :], axis=0
    )
    gram = gram / full

    lat = latents.astype(f32)
    var = jnp.sum(fdot("ti,ik->tk", lat, gram) * lat, axis=1, keepdims=True)
    inv_std = lax.rsqrt(jnp.maximum(var, 0.0) + epsilon)
    lat = (lat * inv_std).reshape(here, SAMPLE_TOKENS, PATCH_DIM)
    centred = fdot("sti,sij->stj", lat, mix)
    wanted = target.reshape(here, SAMPLE_TOKENS, PATCH_DIM).astype(f32)
    output = centred + offset[:, None, :]
    grad_out = (2.0 * (output - wanted) / tok_count).astype(jnp.bfloat16).astype(f32)
    first = jnp.sum(grad_out * gained_mean[:, None, :], axis=2, keepdims=True)
    second = jnp.sum(grad_out * centred, axis=2, keepdims=True) / full
    cross = fdot("sti,stj->sij", lat, grad_out)
    square = fdot("sti,stk->ik", lat * second, lat)
    lean = jnp.sum(lat * first, axis=(0, 1))
    out_sum = jnp.sum(grad_out, axis=1)

    sent = jnp.concatenate(
        [cross.reshape(-1, PATCH_DIM), out_sum, square, lean[None]], axis=0
    )
    got = lax.all_gather(sent, "fsdp")
    cross = got[:, :a].reshape(samples, PATCH_DIM, PATCH_DIM)
    out_sum = got[:, a:b].reshape(samples, PATCH_DIM)
    square = jnp.sum(got[:, b:-1], axis=0)
    lean = jnp.sum(got[:, -1], axis=0)

    centre = wp - mean[:, None]
    turned = fdot("sij,if->sjf", cross, centre)
    grad_head = jnp.sum(turned * gain[:, None, :], axis=0) + fdot("sj,sf->jf", out_sum, shift)
    grad_scale = jnp.sum(turned * wh[None], axis=1)
    grad_shift = fdot("sj,jf->sf", out_sum, wh)
    grad_patch = (
        fdot("sij,sjf->if", cross, gained)
        - lean[:, None]
        - fdot("ik,kf->if", square, centre)
    )
    grad_mod = jnp.stack([jnp.sum(grad_shift, axis=0), jnp.sum(grad_scale, axis=0)])
    grad_pre = ((grad_shift + grad_scale) * silu_slope(pre_act)).astype(jnp.bfloat16)
    grad_time = lax.dot_general(
        sines, grad_pre, (((0,), (0,)), ((), ())), preferred_element_type=f32
    )
    return (
        patch_weight - inner_rate * grad_patch[None],
        head_weight - inner_rate * grad_head[None],
        modulation - inner_rate * grad_mod[None],
        time_weight - inner_rate * grad_time[None],
    )


def per_device(
    latents,
    target,
    timesteps,
    patch_weight,
    head_weight,
    modulation,
    time_weight,
    anchor,
    momentum,
    frag_start,
    frag_current,
):
    inner = (latents, target, timesteps, patch_weight, head_weight, modulation, time_weight)
    fragment = (anchor, momentum, frag_start, frag_current[0])
    fits = anchor.shape[1] % 128 == 0 and timesteps.shape[0] <= 8
    if lax.axis_size("replica") == 8 and 2 <= lax.axis_size("fsdp") <= 4 and fits:
        return window_by_kernel(*inner, *fragment)
    return inner_step(*inner) + tuple(fragment_by_collectives(*fragment))


def solution(mesh):
    in_specs = (
        P(("replica", "fsdp"), None),
        P(("replica", "fsdp"), None),
        P(("replica", "fsdp")),
        P("replica", None, "fsdp"),
        P("replica", None, "fsdp"),
        P("replica", None, "fsdp"),
        P("replica", None, "fsdp"),
        P("fsdp", "replica"),
        P("fsdp", "replica"),
        P("fsdp", None),
        P("replica", "fsdp", None),
    )
    out_specs = (
        P("replica", None, "fsdp"),
        P("replica", None, "fsdp"),
        P("replica", None, "fsdp"),
        P("replica", None, "fsdp"),
        P("fsdp", "replica"),
        P("fsdp", "replica"),
        P("fsdp", None),
    )
    return jax.shard_map(
        per_device, mesh=mesh, in_specs=in_specs, out_specs=out_specs, check_vma=False
    )
```

```python
import math

import jax
import jax.numpy as jnp
from jax import lax
from jax.experimental import pallas as pl
from jax.experimental.pallas import tpu as pltpu
from jax.sharding import PartitionSpec as P

FREQ_DIM = 256
PATCH_DIM = 64
QBLOCK = 128
SAMPLE_TOKENS = 512

epsilon = 1e-06
inner_rate = 0.5
outer_rate = 0.7
momentum_decay = 0.9

MESH = pl.DeviceIdType.MESH
EXACT = lax.Precision.HIGHEST
TIE_UP = 1.0 + 2.0**-22


def sinusoid(time_steps):
    index = jnp.arange(FREQ_DIM // 2, dtype=jnp.float32)
    frequency = jnp.exp(-math.log(10000.0) * index / (FREQ_DIM // 2))
    angles = time_steps.astype(jnp.float32)[:, None] * frequency[None, :]
    return jnp.concatenate([jnp.cos(angles), jnp.sin(angles)], axis=1)


def silu_slope(pre_act):
    sigmoid_val = jax.nn.sigmoid(pre_act)
    return sigmoid_val * (1.0 + pre_act * (1.0 - sigmoid_val))


def fdot(spec, a, b):
    return jnp.einsum(spec, a, b, precision=EXACT, preferred_element_type=jnp.float32)


def nearest(values):
    return lax.round(values, lax.RoundingMethod.TO_NEAREST_EVEN)


def flip(index, bit):
    return index + bit - 2 * bit * lax.rem(index // bit, 2)


def window_kernel(
    blocks,
    cols,
    peers,
    here,
    start_hbm,
    cur_hbm,
    anchor_hbm,
    mom_hbm,
    lat_in,
    target_in,
    sines_in,
    patch_in,
    head_in,
    mod_in,
    time_in,
    patch_out,
    head_out,
    mod_out,
    time_out,
    anchor_out,
    mom_out,
    params_out,
    start_v,
    cur_v,
    terms,
    got1,
    got2,
    got3,
    anchor_v,
    mom_v,
    own,
    load_sem,
    state_sem,
    store_sem,
    s_send,
    s_recv,
    g_send,
    g_recv,
    own_sem,
    sines_all,
    pre,
    gain,
    shift,
    out1,
    in1,
    out2,
    in2,
    total1,
    extra1,
    scale_rows,
    sum_rows,
    z_send,
    z_recv,
):
    f32, bf16 = jnp.float32, jnp.bfloat16
    z = lax.axis_index("fsdp")
    width = patch_in.shape[1]
    full = width * peers
    group = here * PATCH_DIM
    tok_count = here * SAMPLE_TOKENS * peers * 1.0
    me = lax.axis_index("replica")
    core = lax.rem(me, 2)
    rows = QBLOCK
    sibling = flip(me, 1)

    def load(i, slot):
        span = pl.ds(pl.multiple_of(i * rows, rows), rows)
        return (
            pltpu.make_async_copy(start_hbm.at[span, :], start_v.at[slot], load_sem.at[slot, 0]),
            pltpu.make_async_copy(cur_hbm.at[span, :], cur_v.at[slot], load_sem.at[slot, 1]),
        )

    def bits(i):
        first = 2 + 2 * lax.rem(i, 2)
        return first, 6 - first

    def send(src, dst, send_sem, recv_sem, to):
        return pltpu.make_async_remote_copy(
            src_ref=src,
            dst_ref=dst,
            send_sem=send_sem,
            recv_sem=recv_sem,
            device_id={"replica": to},
            device_id_type=MESH,
        )

    def pair_at(who, fixed, other, k):
        chip = who // 2
        f, o = fixed // 2, other // 2
        mine = lax.rem(chip // o, 2)
        return f * lax.rem(chip // f, 2) + o * (mine if k == 1 else 1 - mine)

    def step1(i):
        return send(
            terms.at[i, 1 - core], got1.at[i], s_send.at[0, i], s_recv.at[0, i], sibling
        )

    def step2(i):
        first, second = bits(i)
        to = flip(me, first)
        return [
            send(
                terms.at[i, core, pair_at(to, first, second, k)],
                got2.at[i, k],
                s_send.at[1 + k, i],
                s_recv.at[1 + k, i],
                to,
            )
            for k in range(2)
        ]

    def step3(i):
        first, second = bits(i)
        to = flip(me, second)
        return send(
            terms.at[i, core, to // 2], got3.at[i], s_send.at[3, i], s_recv.at[3, i], to
        )

    def place(i, who):
        span = pl.ds(pl.multiple_of(i * rows, rows), rows)
        return params_out.at[span, pl.ds(pl.multiple_of(who * cols, 128), cols)]

    def back3(i):
        first, second = bits(i)
        return send(
            own.at[i], place(i, me), g_send.at[0, i], g_recv.at[0, i], flip(me, second)
        )

    def back2(i):
        first, second = bits(i)
        to = flip(me, first)
        near = flip(me, second)
        return [
            send(own.at[i], place(i, me), g_send.at[1, i], g_recv.at[1, i], to),
            send(place(i, near), place(i, near), g_send.at[2, i], g_recv.at[2, i], to),
        ]

    def back1(i):
        first, second = bits(i)
        whos = (flip(me, second), flip(me, first), flip(flip(me, first), second))
        sends = [send(own.at[i], place(i, me), g_send.at[3, i], g_recv.at[3, i], sibling)]
        for n, who in enumerate(whos):
            sends.append(
                send(place(i, who), place(i, who), g_send.at[4 + n, i], g_recv.at[4 + n, i], sibling)
            )
        return sends

    def keep(i):
        return pltpu.make_async_copy(own.at[i], place(i, me), own_sem.at[i])

    state_loads = (
        pltpu.make_async_copy(anchor_hbm, anchor_v, state_sem.at[0]),
        pltpu.make_async_copy(mom_hbm, mom_v, state_sem.at[1]),
    )
    for copy in load(0, 0):
        copy.start()
    for copy in state_loads:
        copy.start()

    barrier = pltpu.get_barrier_semaphore()
    for bit in (1, 2, 4):
        pl.semaphore_signal(
            barrier, inc=1, device_id={"replica": flip(me, bit)}, device_id_type=MESH
        )
    for k in range(1, peers):
        pl.semaphore_signal(
            barrier, inc=1, device_id={"fsdp": lax.rem(z + k, peers)}, device_id_type=MESH
        )
    pl.semaphore_wait(barrier, 3 + peers - 1)


    def zsend(src, dst, what, k):
        return pltpu.make_async_remote_copy(
            src_ref=src,
            dst_ref=dst,
            send_sem=z_send.at[what, k - 1],
            recv_sem=z_recv.at[what, k - 1],
            device_id={"fsdp": lax.rem(z + k, peers)},
            device_id_type=MESH,
        )

    def sines_copy(k):
        return zsend(sines_in, sines_all.at[z], 0, k)

    def first_copy(k):
        return zsend(out1.at[k - 1], in1.at[z], 1, k)

    def second_copy(k):
        return zsend(out2, in2.at[z], 2, k)

    def halves(values):
        high = values.astype(bf16)
        return high, (values - high.astype(f32)).astype(bf16)

    def dot(a, b, dims):
        return lax.dot_general(a, b, (dims, ((), ())), preferred_element_type=f32)

    def dot2(a, b, dims):
        high, low = halves(b)
        return dot(a, high, dims) + dot(a, low, dims)

    def dot3(a, b, dims):
        a_high, a_low = halves(a)
        b_high, b_low = halves(b)
        return dot(a_high, b_high, dims) + dot(a_high, b_low, dims) + dot(a_low, b_high, dims)

    nt, nn, tn = ((1,), (1,)), ((1,), (0,)), ((0,), (0,))

    sines_all[z] = sines_in[...]
    for k in range(1, peers):
        sines_copy(k).start()

    def rounded(ref):
        return ref[...].astype(bf16).astype(f32)

    def inner_open():
        for k in range(1, peers):
            sines_copy(k).wait()
        sines = sines_all[...].reshape(peers * 8, FREQ_DIM).astype(bf16)
        pre_act = dot(sines, time_in[...].astype(bf16), nn)
        pre[...] = pre_act
        embed = pre_act * jax.nn.sigmoid(pre_act)
        mod = rounded(mod_in)
        gain[...] = 1.0 + mod[1:2] + embed
        shift[...] = mod[0:1] + embed

    def inner_first(k):
        to = lax.rem(z + k, peers)
        rows8 = pl.ds(pl.multiple_of(to * 8, 8), 8)
        raw = patch_in[...].astype(bf16)
        wp = raw.astype(f32)
        wp = wp - jnp.sum(wp, axis=1, keepdims=True) / width
        wh = rounded(head_in)
        gains = gain[rows8, :]
        parts = [wh * gains[q : q + 1] for q in range(here)]
        gained = jnp.concatenate(parts, axis=0)
        mix = dot3(gained, wp, nt)
        sums = jnp.sum(gained, axis=1, keepdims=True)
        shift_high, shift_low = halves(shift[rows8, :])
        head_bf = wh.astype(bf16)
        offset = dot(head_bf, shift_high, nt) + dot(head_bf, shift_low, nt)
        mean_rows = dot(jnp.ones((8, width), bf16), raw, nt) / width

        def put(ref):
            ref[pl.ds(0, group), 0:64] = mix
            ref[pl.ds(0, group), 64:128] = jnp.broadcast_to(sums, (group, 64))
            ref[pl.ds(group, 64), 0:64] = dot3(wp, wp, nt)
            ref[pl.ds(group, 64), 64:128] = jnp.zeros((64, 64), f32)
            ref[pl.ds(group, 64), 64:72] = offset
            ref[pl.ds(group + 64, 8), 0:64] = mean_rows
            ref[pl.ds(group + 64, 8), 64:128] = jnp.zeros((8, 64), f32)

        if k == 0:
            put(in1.at[z])
        else:
            put(out1.at[k - 1])
            first_copy(k).start()

    def inner_gather():
        for k in range(1, peers):
            first_copy(k).wait()
        means = [in1[d, pl.ds(group + 64, 8), 0:64] for d in range(peers)]
        mean = sum(means[1:], means[0]) / peers
        offs = [m - mean for m in means]
        mix = jnp.zeros((group, 64), f32)
        sums = jnp.zeros((group, 64), f32)
        gram = jnp.zeros((64, 64), f32)
        offset = jnp.zeros((64, 8), f32)
        for d in range(peers):
            wide_sum = in1[d, pl.ds(0, group), 64:128]
            mix = mix + in1[d, pl.ds(0, group), 0:64] + wide_sum * offs[d][0:1]
            sums = sums + wide_sum
            gram = gram + in1[d, pl.ds(group, 64), 0:64]
            gram = gram + (width / 8.0) * dot3(offs[d], offs[d], tn)
            offset = offset + in1[d, pl.ds(group, 64), 64:72]
        total1[pl.ds(0, group), 0:64] = mix
        total1[pl.ds(0, group), 64:128] = sums / full
        total1[pl.ds(group, 64), 0:64] = gram / full
        total1[pl.ds(group, 64), 64:128] = dot2(jnp.ones((64, 8), bf16), mean, nn).T / 8.0
        extra1[:, 0:8] = offset
        out2[...] = jnp.zeros_like(out2)

    def inner_sample(q):
        span = pl.ds(q * SAMPLE_TOKENS, SAMPLE_TOKENS)
        at = pl.ds(q * PATCH_DIM, PATCH_DIM)
        lat_bf = lat_in[:, span]
        lat = lat_bf.astype(f32)
        gram_high, gram_low = halves(total1[pl.ds(group, 64), 0:64])
        mix_high, mix_low = halves(total1[at, 0:64])
        spread = dot(gram_high, lat_bf, nn) + dot(gram_low, lat_bf, nn)
        var = jnp.sum(spread * lat, axis=0, keepdims=True)
        inv_std = lax.rsqrt(jnp.maximum(var, 0.0) + epsilon)
        centred = (dot(mix_high, lat_bf, nn) + dot(mix_low, lat_bf, nn)) * inv_std
        output = centred + extra1[:, q : q + 1]
        grad_out = (2.0 * (output - target_in[:, span].astype(f32)) / tok_count).astype(bf16)
        grad_f = grad_out.astype(f32)
        first = jnp.sum(grad_f * total1[at, 64:65], axis=0, keepdims=True)
        second = jnp.sum(grad_f * centred, axis=0, keepdims=True) / full
        lat = lat * inv_std
        out2[at, 0:64] = dot2(grad_out, lat, nt)
        out2[pl.ds(group, 64), 0:64] += dot3(lat, lat * second, nt)
        lean = jnp.sum(lat * first, axis=1, keepdims=True)
        out2[pl.ds(group, 64), 64:128] += jnp.broadcast_to(lean, (64, 64))
        sums = dot(jnp.ones((8, SAMPLE_TOKENS), bf16), grad_out, nt)
        out2[pl.ds(group + 64 + q, 1), 0:64] = sums[0:1]

    def inner_second():
        in2[z] = out2[...]
        for k in range(1, peers):
            second_copy(k).start()

    def inner_close():
        for k in range(1, peers):
            second_copy(k).wait()
        rest = in2[0, pl.ds(group, 64), :]
        for d in range(1, peers):
            rest = rest + in2[d, pl.ds(group, 64), :]
        centre = rounded(patch_in) - total1[pl.ds(group, 64), 64:65]
        patch_out[...] = patch_in[...] + inner_rate * (
            rest[:, 64:65] + dot3(rest[:, 0:64], centre, nn)
        )
        for d in range(peers):
            sum_rows[pl.ds(8 * d, 8), :] = in2[d, pl.ds(group + 64, 8), 0:64]
        head_out[...] = head_in[...] - inner_rate * dot3(sum_rows[...], shift[...], tn)
        scale_rows[...] = jnp.zeros_like(scale_rows)

    def inner_source(d):
        centre = rounded(patch_in) - total1[pl.ds(group, 64), 64:65]
        wh = rounded(head_in)
        cross = in2[d, pl.ds(0, group), 0:64]
        turned = dot3(cross, centre, nn)
        parts = []
        head_sum = jnp.zeros_like(wh)
        for q in range(here):
            row = gain[8 * d + q : 8 * d + q + 1, :]
            piece = turned[q * 64 : q * 64 + 64]
            head_sum = head_sum + piece * row
            scale_rows[8 * d + q : 8 * d + q + 1, :] = jnp.sum(piece * wh, axis=0, keepdims=True)
            parts.append(wh * row)
        head_out[...] -= inner_rate * head_sum
        patch_out[...] -= inner_rate * dot3(cross, jnp.concatenate(parts, axis=0), tn)

    def inner_end():
        grad_scale = scale_rows[...]
        high, low = halves(sum_rows[...])
        head_bf = head_in[...].astype(bf16)
        grad_shift = dot(high, head_bf, nn) + dot(low, head_bf, nn)
        mod_out[0:1, :] = mod_in[0:1, :] - inner_rate * jnp.sum(grad_shift, axis=0, keepdims=True)
        mod_out[1:2, :] = mod_in[1:2, :] - inner_rate * jnp.sum(grad_scale, axis=0, keepdims=True)
        sines = sines_all[...].reshape(peers * 8, FREQ_DIM).astype(bf16)
        grad_pre = ((grad_shift + grad_scale) * silu_slope(pre[...])).astype(bf16)
        time_out[...] = time_in[...] - inner_rate * dot(sines, grad_pre, tn)

    def quantize(i):
        slot = lax.rem(i, 2)
        for copy in load(i, slot):
            copy.wait()

        @pl.when(i + 1 < blocks)
        def _():
            for copy in load(i + 1, 1 - slot):
                copy.start()

        for who in range(8):
            for part in range(cols // 128):
                lanes = pl.ds(who * cols + part * 128, 128)
                delta = start_v[slot, :, lanes].astype(jnp.float32) - cur_v[
                    slot, :, lanes
                ].astype(jnp.float32)
                top = jnp.max(jnp.abs(delta), axis=0, keepdims=True)
                scale = (top + epsilon).astype(jnp.bfloat16).astype(jnp.float32)
                level = nearest(delta * (7.0 * TIE_UP / scale))
                level = jnp.clip(level, -7.0, 7.0)
                terms[i, who % 2, who // 2, :, pl.ds(part * 128, 128)] = (
                    level * (scale / 7.0)
                ).astype(jnp.bfloat16)
        step1(i).start()

    def fold1(i):
        step1(i).wait()
        for k in range(4):
            terms[i, core, k] = (
                terms[i, core, k].astype(jnp.float32) + got1[i, k].astype(jnp.float32)
            ).astype(jnp.bfloat16)
        for copy in step2(i):
            copy.start()

    def fold2(i):
        first, second = bits(i)
        for k, copy in enumerate(step2(i)):
            copy.wait()
            at = pair_at(me, first, second, k)
            terms[i, core, at] = (
                terms[i, core, at].astype(jnp.float32) + got2[i, k].astype(jnp.float32)
            ).astype(jnp.bfloat16)
            if k == 0:
                step3(i).start()

    def update(i):
        step3(i).wait()

        @pl.when(i == 0)
        def _():
            for copy in state_loads:
                copy.wait()

        span = pl.ds(pl.multiple_of(i * rows, rows), rows)
        average = (
            terms[i, core, me // 2].astype(jnp.float32) + got3[i].astype(jnp.float32)
        ) / 8.0
        new_momentum = momentum_decay * mom_v[span, :] + average
        new_anchor = anchor_v[span, :] - outer_rate * (average + momentum_decay * new_momentum)
        mom_v[span, :] = new_momentum
        anchor_v[span, :] = new_anchor
        own[i] = new_anchor.astype(jnp.bfloat16)
        back3(i).start()
        back2(i)[0].start()
        back1(i)[0].start()
        keep(i).start()
        pltpu.make_async_copy(anchor_v.at[span, :], anchor_out.at[span, :], store_sem.at[0, i]).start()
        pltpu.make_async_copy(mom_v.at[span, :], mom_out.at[span, :], store_sem.at[1, i]).start()

    def spread2(i):
        back3(i).wait()
        back2(i)[1].start()
        back1(i)[1].start()

    def spread1(i):
        for n, copy in enumerate(back2(i)):
            copy.wait()
            back1(i)[2 + n].start()

    stages = ((9, spread1), (7, spread2), (5, update), (0, quantize), (1, fold1), (3, fold2))
    last = max(lag for lag, _ in stages)

    parts = [(2, inner_open)]
    parts += [(3 + k, lambda k=k: inner_first(peers - 1 - k)) for k in range(peers)]
    at = 5 + peers
    parts += [(at, inner_gather)]
    parts += [(at + q, lambda q=q: inner_sample(q)) for q in range(here)]
    at += here
    parts += [(at - 1, inner_second), (at + 1, inner_close)]
    parts += [(at + 1 + d, lambda d=d: inner_source(d)) for d in range(peers)]
    parts += [(at + 1 + peers, inner_end)]

    def step(i, carry):
        for lag, stage in stages:

            @pl.when(jnp.logical_and(i >= lag, i < blocks + lag))
            def _(stage=stage, lag=lag):
                stage(i - lag)

        for when, part in parts:

            @pl.when(i == when)
            def _(part=part):
                part()

        return carry

    lax.fori_loop(0, max(blocks + last, parts[-1][0] + 1), step, 0)

    def finish(i, carry):
        span = pl.ds(pl.multiple_of(i * rows, rows), rows)
        for copy in back1(i):
            copy.wait()
        keep(i).wait()
        pltpu.make_async_copy(anchor_v.at[span, :], anchor_out.at[span, :], store_sem.at[0, i]).wait()
        pltpu.make_async_copy(mom_v.at[span, :], mom_out.at[span, :], store_sem.at[1, i]).wait()
        return carry

    lax.fori_loop(0, blocks, finish, 0)


def hand_on(arrays):
    pieces = []
    for n, a in enumerate(arrays):
        rows = a.shape[0]
        size = QBLOCK if rows % QBLOCK == 0 else rows
        pieces += [(n, at, size) for at in range(0, rows, size)]

    def kernel(*refs):
        count = len(arrays)
        ins, outs, held = refs[:count], refs[count : 2 * count], refs[2 * count : 3 * count]
        load_sem, store_sem = refs[3 * count :]

        def moves(k):
            n, at, size = pieces[k]
            rows = pl.ds(at, size)
            return (
                pltpu.make_async_copy(ins[n].at[rows], held[n].at[rows], load_sem.at[k]),
                pltpu.make_async_copy(held[n].at[rows], outs[n].at[rows], store_sem.at[k]),
            )

        for k in range(len(pieces)):
            moves(k)[0].start()
        for k in range(len(pieces)):
            moves(k)[0].wait()
            moves(k)[1].start()
        for k in range(len(pieces)):
            moves(k)[1].wait()

    dma = pltpu.SemaphoreType.DMA
    return pl.pallas_call(
        kernel,
        out_shape=tuple(jax.ShapeDtypeStruct(a.shape, a.dtype) for a in arrays),
        in_specs=[pl.BlockSpec(memory_space=pl.ANY)] * len(arrays),
        out_specs=(pl.BlockSpec(memory_space=pl.ANY),) * len(arrays),
        scratch_shapes=[pltpu.VMEM(a.shape, a.dtype) for a in arrays]
        + [dma((len(pieces),)), dma((len(pieces),))],
        compiler_params=pltpu.CompilerParams(vmem_limit_bytes=60 * 1024 * 1024),
        name="hand_on",
    )(*arrays)


def window_by_kernel(
    latents,
    target,
    timesteps,
    patch_weight,
    head_weight,
    modulation,
    time_weight,
    anchor,
    momentum,
    frag_start,
    frag_current,
):
    rows, span = frag_start.shape
    blocks, cols = rows // QBLOCK, anchor.shape[1]
    peers, here = lax.axis_size("fsdp"), timesteps.shape[0]
    width = patch_weight.shape[2]
    group = here * PATCH_DIM
    bf16, f32 = jnp.bfloat16, jnp.float32
    dma = pltpu.SemaphoreType.DMA
    sines = lax.reduce_precision(sinusoid(timesteps), 8, 7)
    sines = jnp.pad(sines, ((0, 8 - here), (0, 0)))
    params = (patch_weight[0], head_weight[0], modulation[0], time_weight[0])
    out = pl.pallas_call(
        lambda *refs: window_kernel(blocks, cols, peers, here, *refs),
        out_shape=tuple(jax.ShapeDtypeStruct(p.shape, f32) for p in params)
        + (
            jax.ShapeDtypeStruct((rows, cols), f32),
            jax.ShapeDtypeStruct((rows, cols), f32),
            jax.ShapeDtypeStruct((rows, span), bf16),
        ),
        in_specs=[pl.BlockSpec(memory_space=pl.ANY)] * 4
        + [pl.BlockSpec(memory_space=pltpu.VMEM)] * 7,
        out_specs=(pl.BlockSpec(memory_space=pltpu.VMEM),) * 4
        + (pl.BlockSpec(memory_space=pl.ANY),) * 3,
        scratch_shapes=[
            pltpu.VMEM((2, QBLOCK, span), bf16),
            pltpu.VMEM((2, QBLOCK, span), bf16),
            pltpu.VMEM((blocks, 2, 4, QBLOCK, cols), bf16),
            pltpu.VMEM((blocks, 4, QBLOCK, cols), bf16),
            pltpu.VMEM((blocks, 2, QBLOCK, cols), bf16),
            pltpu.VMEM((blocks, QBLOCK, cols), bf16),
            pltpu.VMEM((rows, cols), f32),
            pltpu.VMEM((rows, cols), f32),
            pltpu.VMEM((blocks, QBLOCK, cols), bf16),
            dma((2, 2)),
            dma((2,)),
            dma((2, blocks)),
            dma((4, blocks)),
            dma((4, blocks)),
            dma((7, blocks)),
            dma((7, blocks)),
            dma((blocks,)),
            pltpu.VMEM((peers, 8, FREQ_DIM), f32),
            pltpu.VMEM((peers * 8, width), f32),
            pltpu.VMEM((peers * 8, width), f32),
            pltpu.VMEM((peers * 8, width), f32),
            pltpu.VMEM((peers - 1, group + 72, 128), f32),
            pltpu.VMEM((peers, group + 72, 128), f32),
            pltpu.VMEM((group + 72, 128), f32),
            pltpu.VMEM((peers, group + 72, 128), f32),
            pltpu.VMEM((group + 64, 128), f32),
            pltpu.VMEM((64, 128), f32),
            pltpu.VMEM((peers * 8, width), f32),
            pltpu.VMEM((peers * 8, 64), f32),
            dma((3, peers - 1)),
            dma((3, peers - 1)),
        ],
        compiler_params=pltpu.CompilerParams(
            collective_id=0, has_side_effects=True, vmem_limit_bytes=60 * 1024 * 1024
        ),
        cost_estimate=pl.CostEstimate(
            flops=20 * rows * span, bytes_accessed=8 * rows * span, transcendentals=0
        ),
        name="window",
    )(frag_start, frag_current, anchor, momentum, latents.T, target.T, sines, *params)
    out = hand_on(out)
    return tuple(o[None] for o in out[:4]) + tuple(out[4:])


def fragment_by_collectives(anchor, momentum, frag_start, frag_current):
    replica_count = lax.axis_size("replica")
    delta = frag_start.astype(jnp.float32) - frag_current.astype(jnp.float32)
    rows, width = delta.shape
    blocks = delta.reshape(rows // QBLOCK, QBLOCK, width)
    top = jnp.max(jnp.abs(blocks), axis=1, keepdims=True)
    scale = lax.reduce_precision(top + epsilon, 8, 7)
    level = jnp.clip(nearest(blocks * (7.0 * TIE_UP / scale)), -7.0, 7.0)
    terms = (level * (scale / 7.0)).astype(jnp.bfloat16).reshape(rows, width)
    total = lax.psum_scatter(terms, "replica", scatter_dimension=1, tiled=True)
    average = total.astype(jnp.float32) / replica_count
    new_momentum = momentum_decay * momentum + average
    new_anchor = anchor - outer_rate * (average + momentum_decay * new_momentum)
    new_params = lax.all_gather(new_anchor.astype(jnp.bfloat16), "replica", axis=1, tiled=True)
    return new_anchor, new_momentum, new_params


def inner_step(latents, target, timesteps, patch_weight, head_weight, modulation, time_weight):
    fsdp = lax.axis_size("fsdp")
    here = timesteps.shape[0]
    samples = here * fsdp
    width = patch_weight.shape[2]
    full = width * fsdp
    tok_count = latents.shape[0] * fsdp * 1.0
    f32 = jnp.float32

    sines = sinusoid(lax.all_gather(timesteps, "fsdp", tiled=True)).astype(jnp.bfloat16)
    wp = patch_weight[0].astype(jnp.bfloat16).astype(f32)
    wh = head_weight[0].astype(jnp.bfloat16).astype(f32)
    wm = modulation[0].astype(jnp.bfloat16).astype(f32)
    pre_act = jnp.dot(sines, time_weight[0].astype(jnp.bfloat16), preferred_element_type=f32)
    embed = jax.nn.silu(pre_act)
    gain = 1.0 + wm[1] + embed
    shift = wm[0] + embed

    mean_here = jnp.mean(wp, axis=1)
    wp_here = wp - mean_here[:, None]
    gained = wh[None] * gain[:, None, :]
    gram = fdot("if,kf->ik", wp_here, wp_here)
    mix = fdot("sjf,if->sij", gained, wp_here)
    gained_sum = jnp.sum(gained, axis=2)
    offset = fdot("sf,jf->sj", shift, wh)

    def split(a):
        return a.reshape(fsdp, -1, PATCH_DIM)

    def copies(a):
        return jnp.broadcast_to(a.reshape(1, -1, PATCH_DIM), (fsdp, a.size // PATCH_DIM, PATCH_DIM))

    sent = jnp.concatenate(
        [split(mix), split(gained_sum), split(offset), copies(gram), copies(mean_here)], axis=1
    )
    got = lax.all_to_all(sent, "fsdp", 0, 0)
    a, b = here * PATCH_DIM, here * PATCH_DIM + here
    mean_of = got[:, -1]
    mean = jnp.mean(mean_of, axis=0)
    off_mean = mean_of - mean
    gained_sum_of = got[:, a:b]
    mix = jnp.sum(got[:, :a], axis=0).reshape(here, PATCH_DIM, PATCH_DIM) + jnp.sum(
        off_mean[:, None, :, None] * gained_sum_of[:, :, None, :], axis=0
    )
    gained_mean = jnp.sum(gained_sum_of, axis=0) / full
    offset = jnp.sum(got[:, b : b + here], axis=0)
    gram = jnp.sum(got[:, b + here : -1], axis=0) + width * jnp.sum(
        off_mean[:, :, None] * off_mean[:, None, :], axis=0
    )
    gram = gram / full

    lat = latents.astype(f32)
    var = jnp.sum(fdot("ti,ik->tk", lat, gram) * lat, axis=1, keepdims=True)
    inv_std = lax.rsqrt(jnp.maximum(var, 0.0) + epsilon)
    lat = (lat * inv_std).reshape(here, SAMPLE_TOKENS, PATCH_DIM)
    centred = fdot("sti,sij->stj", lat, mix)
    wanted = target.reshape(here, SAMPLE_TOKENS, PATCH_DIM).astype(f32)
    output = centred + offset[:, None, :]
    grad_out = (2.0 * (output - wanted) / tok_count).astype(jnp.bfloat16).astype(f32)
    first = jnp.sum(grad_out * gained_mean[:, None, :], axis=2, keepdims=True)
    second = jnp.sum(grad_out * centred, axis=2, keepdims=True) / full
    cross = fdot("sti,stj->sij", lat, grad_out)
    square = fdot("sti,stk->ik", lat * second, lat)
    lean = jnp.sum(lat * first, axis=(0, 1))
    out_sum = jnp.sum(grad_out, axis=1)

    sent = jnp.concatenate(
        [cross.reshape(-1, PATCH_DIM), out_sum, square, lean[None]], axis=0
    )
    got = lax.all_gather(sent, "fsdp")
    cross = got[:, :a].reshape(samples, PATCH_DIM, PATCH_DIM)
    out_sum = got[:, a:b].reshape(samples, PATCH_DIM)
    square = jnp.sum(got[:, b:-1], axis=0)
    lean = jnp.sum(got[:, -1], axis=0)

    centre = wp - mean[:, None]
    turned = fdot("sij,if->sjf", cross, centre)
    grad_head = jnp.sum(turned * gain[:, None, :], axis=0) + fdot("sj,sf->jf", out_sum, shift)
    grad_scale = jnp.sum(turned * wh[None], axis=1)
    grad_shift = fdot("sj,jf->sf", out_sum, wh)
    grad_patch = (
        fdot("sij,sjf->if", cross, gained)
        - lean[:, None]
        - fdot("ik,kf->if", square, centre)
    )
    grad_mod = jnp.stack([jnp.sum(grad_shift, axis=0), jnp.sum(grad_scale, axis=0)])
    grad_pre = ((grad_shift + grad_scale) * silu_slope(pre_act)).astype(jnp.bfloat16)
    grad_time = lax.dot_general(
        sines, grad_pre, (((0,), (0,)), ((), ())), preferred_element_type=f32
    )
    return (
        patch_weight - inner_rate * grad_patch[None],
        head_weight - inner_rate * grad_head[None],
        modulation - inner_rate * grad_mod[None],
        time_weight - inner_rate * grad_time[None],
    )


def per_device(
    latents,
    target,
    timesteps,
    patch_weight,
    head_weight,
    modulation,
    time_weight,
    anchor,
    momentum,
    frag_start,
    frag_current,
):
    inner = (latents, target, timesteps, patch_weight, head_weight, modulation, time_weight)
    fragment = (anchor, momentum, frag_start, frag_current[0])
    fits = anchor.shape[1] % 128 == 0 and timesteps.shape[0] <= 8
    if lax.axis_size("replica") == 8 and 2 <= lax.axis_size("fsdp") <= 4 and fits:
        return window_by_kernel(*inner, *fragment)
    return inner_step(*inner) + tuple(fragment_by_collectives(*fragment))


def solution(mesh):
    in_specs = (
        P(("replica", "fsdp"), None),
        P(("replica", "fsdp"), None),
        P(("replica", "fsdp")),
        P("replica", None, "fsdp"),
        P("replica", None, "fsdp"),
        P("replica", None, "fsdp"),
        P("replica", None, "fsdp"),
        P("fsdp", "replica"),
        P("fsdp", "replica"),
        P("fsdp", None),
        P("replica", "fsdp", None),
    )
    out_specs = (
        P("replica", None, "fsdp"),
        P("replica", None, "fsdp"),
        P("replica", None, "fsdp"),
        P("replica", None, "fsdp"),
        P("fsdp", "replica"),
        P("fsdp", "replica"),
        P("fsdp", None),
    )
    return jax.shard_map(
        per_device, mesh=mesh, in_specs=in_specs, out_specs=out_specs, check_vma=False
    )
```

```python
import math

import jax
import jax.numpy as jnp
from jax import lax
from jax.experimental import pallas as pl
from jax.experimental.pallas import tpu as pltpu
from jax.sharding import PartitionSpec as P

FREQ_DIM = 256
PATCH_DIM = 64
QBLOCK = 128
SAMPLE_TOKENS = 512

epsilon = 1e-06
inner_rate = 0.5
outer_rate = 0.7
momentum_decay = 0.9

MESH = pl.DeviceIdType.MESH
EXACT = lax.Precision.HIGHEST
TIE_UP = 1.0 + 2.0**-22


def sinusoid(time_steps):
    index = jnp.arange(FREQ_DIM // 2, dtype=jnp.float32)
    frequency = jnp.exp(-math.log(10000.0) * index / (FREQ_DIM // 2))
    angles = time_steps.astype(jnp.float32)[:, None] * frequency[None, :]
    return jnp.concatenate([jnp.cos(angles), jnp.sin(angles)], axis=1)


def silu_slope(pre_act):
    sigmoid_val = jax.nn.sigmoid(pre_act)
    return sigmoid_val * (1.0 + pre_act * (1.0 - sigmoid_val))


def fdot(spec, a, b):
    return jnp.einsum(spec, a, b, precision=EXACT, preferred_element_type=jnp.float32)


def nearest(values):
    return lax.round(values, lax.RoundingMethod.TO_NEAREST_EVEN)


def flip(index, bit):
    return index + bit - 2 * bit * lax.rem(index // bit, 2)


def window_kernel(
    blocks,
    cols,
    peers,
    here,
    start_hbm,
    cur_hbm,
    anchor_hbm,
    mom_hbm,
    lat_in,
    target_in,
    sines_in,
    patch_in,
    head_in,
    mod_in,
    time_in,
    patch_out,
    head_out,
    mod_out,
    time_out,
    anchor_out,
    mom_out,
    params_out,
    start_v,
    cur_v,
    terms,
    got1,
    got2,
    got3,
    anchor_v,
    mom_v,
    own,
    load_sem,
    state_sem,
    store_sem,
    s_send,
    s_recv,
    g_send,
    g_recv,
    own_sem,
    sines_all,
    pre,
    gain,
    shift,
    out1,
    in1,
    out2,
    in2,
    total1,
    extra1,
    scale_rows,
    sum_rows,
    z_send,
    z_recv,
):
    f32, bf16 = jnp.float32, jnp.bfloat16
    z = lax.axis_index("fsdp")
    width = patch_in.shape[1]
    full = width * peers
    group = here * PATCH_DIM
    tok_count = here * SAMPLE_TOKENS * peers * 1.0
    me = lax.axis_index("replica")
    core = lax.rem(me, 2)
    rows = QBLOCK
    sibling = flip(me, 1)

    def load(i, slot):
        span = pl.ds(pl.multiple_of(i * rows, rows), rows)
        return (
            pltpu.make_async_copy(start_hbm.at[span, :], start_v.at[slot], load_sem.at[slot, 0]),
            pltpu.make_async_copy(cur_hbm.at[span, :], cur_v.at[slot], load_sem.at[slot, 1]),
        )

    def bits(i):
        first = 2 + 2 * lax.rem(i, 2)
        return first, 6 - first

    def send(src, dst, send_sem, recv_sem, to):
        return pltpu.make_async_remote_copy(
            src_ref=src,
            dst_ref=dst,
            send_sem=send_sem,
            recv_sem=recv_sem,
            device_id={"replica": to},
            device_id_type=MESH,
        )

    def pair_at(who, fixed, other, k):
        chip = who // 2
        f, o = fixed // 2, other // 2
        mine = lax.rem(chip // o, 2)
        return f * lax.rem(chip // f, 2) + o * (mine if k == 1 else 1 - mine)

    def step1(i):
        return send(
            terms.at[i, 1 - core], got1.at[i], s_send.at[0, i], s_recv.at[0, i], sibling
        )

    def step2(i):
        first, second = bits(i)
        to = flip(me, first)
        return [
            send(
                terms.at[i, core, pair_at(to, first, second, k)],
                got2.at[i, k],
                s_send.at[1 + k, i],
                s_recv.at[1 + k, i],
                to,
            )
            for k in range(2)
        ]

    def step3(i):
        first, second = bits(i)
        to = flip(me, second)
        return send(
            terms.at[i, core, to // 2], got3.at[i], s_send.at[3, i], s_recv.at[3, i], to
        )

    def place(i, who):
        span = pl.ds(pl.multiple_of(i * rows, rows), rows)
        return params_out.at[span, pl.ds(pl.multiple_of(who * cols, 128), cols)]

    def back3(i):
        first, second = bits(i)
        return send(
            own.at[i], place(i, me), g_send.at[0, i], g_recv.at[0, i], flip(me, second)
        )

    def back2(i):
        first, second = bits(i)
        to = flip(me, first)
        near = flip(me, second)
        return [
            send(own.at[i], place(i, me), g_send.at[1, i], g_recv.at[1, i], to),
            send(place(i, near), place(i, near), g_send.at[2, i], g_recv.at[2, i], to),
        ]

    def back1(i):
        first, second = bits(i)
        whos = (flip(me, second), flip(me, first), flip(flip(me, first), second))
        sends = [send(own.at[i], place(i, me), g_send.at[3, i], g_recv.at[3, i], sibling)]
        for n, who in enumerate(whos):
            sends.append(
                send(place(i, who), place(i, who), g_send.at[4 + n, i], g_recv.at[4 + n, i], sibling)
            )
        return sends

    def keep(i):
        return pltpu.make_async_copy(own.at[i], place(i, me), own_sem.at[i])

    state_loads = (
        pltpu.make_async_copy(anchor_hbm, anchor_v, state_sem.at[0]),
        pltpu.make_async_copy(mom_hbm, mom_v, state_sem.at[1]),
    )
    for copy in load(0, 0):
        copy.start()
    for copy in state_loads:
        copy.start()

    barrier = pltpu.get_barrier_semaphore()
    for bit in (1, 2, 4):
        pl.semaphore_signal(
            barrier, inc=1, device_id={"replica": flip(me, bit)}, device_id_type=MESH
        )
    for k in range(1, peers):
        pl.semaphore_signal(
            barrier, inc=1, device_id={"fsdp": lax.rem(z + k, peers)}, device_id_type=MESH
        )
    pl.semaphore_wait(barrier, 3 + peers - 1)


    def zsend(src, dst, what, k):
        return pltpu.make_async_remote_copy(
            src_ref=src,
            dst_ref=dst,
            send_sem=z_send.at[what, k - 1],
            recv_sem=z_recv.at[what, k - 1],
            device_id={"fsdp": lax.rem(z + k, peers)},
            device_id_type=MESH,
        )

    def sines_copy(k):
        return zsend(sines_in, sines_all.at[z], 0, k)

    def first_copy(k):
        return zsend(out1.at[k - 1], in1.at[z], 1, k)

    def second_copy(k):
        return zsend(out2, in2.at[z], 2, k)

    def halves(values):
        high = values.astype(bf16)
        return high, (values - high.astype(f32)).astype(bf16)

    def dot(a, b, dims):
        return lax.dot_general(a, b, (dims, ((), ())), preferred_element_type=f32)

    def dot2(a, b, dims):
        high, low = halves(b)
        return dot(a, high, dims) + dot(a, low, dims)

    def dot3(a, b, dims):
        a_high, a_low = halves(a)
        b_high, b_low = halves(b)
        return dot(a_high, b_high, dims) + dot(a_high, b_low, dims) + dot(a_low, b_high, dims)

    nt, nn, tn = ((1,), (1,)), ((1,), (0,)), ((0,), (0,))

    sines_all[z] = sines_in[...]
    for k in range(1, peers):
        sines_copy(k).start()

    def rounded(ref):
        return ref[...].astype(bf16).astype(f32)

    def inner_open():
        for k in range(1, peers):
            sines_copy(k).wait()
        sines = sines_all[...].reshape(peers * 8, FREQ_DIM).astype(bf16)
        pre_act = dot(sines, time_in[...].astype(bf16), nn)
        pre[...] = pre_act
        embed = pre_act * jax.nn.sigmoid(pre_act)
        mod = rounded(mod_in)
        gain[...] = 1.0 + mod[1:2] + embed
        shift[...] = mod[0:1] + embed

    def inner_first(k):
        to = lax.rem(z + k, peers)
        rows8 = pl.ds(pl.multiple_of(to * 8, 8), 8)
        raw = patch_in[...].astype(bf16)
        wp = raw.astype(f32)
        wp = wp - jnp.sum(wp, axis=1, keepdims=True) / width
        wh = rounded(head_in)
        gains = gain[rows8, :]
        parts = [wh * gains[q : q + 1] for q in range(here)]
        gained = jnp.concatenate(parts, axis=0)
        mix = dot3(gained, wp, nt)
        sums = jnp.sum(gained, axis=1, keepdims=True)
        shift_high, shift_low = halves(shift[rows8, :])
        head_bf = wh.astype(bf16)
        offset = dot(head_bf, shift_high, nt) + dot(head_bf, shift_low, nt)
        mean_rows = dot(jnp.ones((8, width), bf16), raw, nt) / width

        def put(ref):
            ref[pl.ds(0, group), 0:64] = mix
            ref[pl.ds(0, group), 64:128] = jnp.broadcast_to(sums, (group, 64))
            ref[pl.ds(group, 64), 0:64] = dot3(wp, wp, nt)
            ref[pl.ds(group, 64), 64:128] = jnp.zeros((64, 64), f32)
            ref[pl.ds(group, 64), 64:72] = offset
            ref[pl.ds(group + 64, 8), 0:64] = mean_rows
            ref[pl.ds(group + 64, 8), 64:128] = jnp.zeros((8, 64), f32)

        if k == 0:
            put(in1.at[z])
        else:
            put(out1.at[k - 1])
            first_copy(k).start()

    def inner_gather():
        for k in range(1, peers):
            first_copy(k).wait()
        means = [in1[d, pl.ds(group + 64, 8), 0:64] for d in range(peers)]
        mean = sum(means[1:], means[0]) / peers
        offs = [m - mean for m in means]
        mix = jnp.zeros((group, 64), f32)
        sums = jnp.zeros((group, 64), f32)
        gram = jnp.zeros((64, 64), f32)
        offset = jnp.zeros((64, 8), f32)
        for d in range(peers):
            wide_sum = in1[d, pl.ds(0, group), 64:128]
            mix = mix + in1[d, pl.ds(0, group), 0:64] + wide_sum * offs[d][0:1]
            sums = sums + wide_sum
            gram = gram + in1[d, pl.ds(group, 64), 0:64]
            gram = gram + (width / 8.0) * dot3(offs[d], offs[d], tn)
            offset = offset + in1[d, pl.ds(group, 64), 64:72]
        total1[pl.ds(0, group), 0:64] = mix
        total1[pl.ds(0, group), 64:128] = sums / full
        total1[pl.ds(group, 64), 0:64] = gram / full
        total1[pl.ds(group, 64), 64:128] = dot2(jnp.ones((64, 8), bf16), mean, nn).T / 8.0
        extra1[:, 0:8] = offset
        out2[...] = jnp.zeros_like(out2)

    def inner_sample(q):
        span = pl.ds(q * SAMPLE_TOKENS, SAMPLE_TOKENS)
        at = pl.ds(q * PATCH_DIM, PATCH_DIM)
        lat_bf = lat_in[:, span]
        lat = lat_bf.astype(f32)
        gram_high, gram_low = halves(total1[pl.ds(group, 64), 0:64])
        mix_high, mix_low = halves(total1[at, 0:64])
        spread = dot(gram_high, lat_bf, nn) + dot(gram_low, lat_bf, nn)
        var = jnp.sum(spread * lat, axis=0, keepdims=True)
        inv_std = lax.rsqrt(jnp.maximum(var, 0.0) + epsilon)
        centred = (dot(mix_high, lat_bf, nn) + dot(mix_low, lat_bf, nn)) * inv_std
        output = centred + extra1[:, q : q + 1]
        grad_out = (2.0 * (output - target_in[:, span].astype(f32)) / tok_count).astype(bf16)
        grad_f = grad_out.astype(f32)
        first = jnp.sum(grad_f * total1[at, 64:65], axis=0, keepdims=True)
        second = jnp.sum(grad_f * centred, axis=0, keepdims=True) / full
        lat = lat * inv_std
        out2[at, 0:64] = dot2(grad_out, lat, nt)
        out2[pl.ds(group, 64), 0:64] += dot3(lat, lat * second, nt)
        lean = jnp.sum(lat * first, axis=1, keepdims=True)
        out2[pl.ds(group, 64), 64:128] += jnp.broadcast_to(lean, (64, 64))
        sums = dot(jnp.ones((8, SAMPLE_TOKENS), bf16), grad_out, nt)
        out2[pl.ds(group + 64 + q, 1), 0:64] = sums[0:1]

    def inner_second():
        in2[z] = out2[...]
        for k in range(1, peers):
            second_copy(k).start()

    def inner_close():
        for k in range(1, peers):
            second_copy(k).wait()
        rest = in2[0, pl.ds(group, 64), :]
        for d in range(1, peers):
            rest = rest + in2[d, pl.ds(group, 64), :]
        centre = rounded(patch_in) - total1[pl.ds(group, 64), 64:65]
        patch_out[...] = patch_in[...] + inner_rate * (
            rest[:, 64:65] + dot3(rest[:, 0:64], centre, nn)
        )
        for d in range(peers):
            sum_rows[pl.ds(8 * d, 8), :] = in2[d, pl.ds(group + 64, 8), 0:64]
        head_out[...] = head_in[...] - inner_rate * dot3(sum_rows[...], shift[...], tn)
        scale_rows[...] = jnp.zeros_like(scale_rows)

    def inner_source(d):
        centre = rounded(patch_in) - total1[pl.ds(group, 64), 64:65]
        wh = rounded(head_in)
        cross = in2[d, pl.ds(0, group), 0:64]
        turned = dot3(cross, centre, nn)
        parts = []
        head_sum = jnp.zeros_like(wh)
        for q in range(here):
            row = gain[8 * d + q : 8 * d + q + 1, :]
            piece = turned[q * 64 : q * 64 + 64]
            head_sum = head_sum + piece * row
            scale_rows[8 * d + q : 8 * d + q + 1, :] = jnp.sum(piece * wh, axis=0, keepdims=True)
            parts.append(wh * row)
        head_out[...] -= inner_rate * head_sum
        patch_out[...] -= inner_rate * dot3(cross, jnp.concatenate(parts, axis=0), tn)

    def inner_end():
        grad_scale = scale_rows[...]
        high, low = halves(sum_rows[...])
        head_bf = head_in[...].astype(bf16)
        grad_shift = dot(high, head_bf, nn) + dot(low, head_bf, nn)
        mod_out[0:1, :] = mod_in[0:1, :] - inner_rate * jnp.sum(grad_shift, axis=0, keepdims=True)
        mod_out[1:2, :] = mod_in[1:2, :] - inner_rate * jnp.sum(grad_scale, axis=0, keepdims=True)
        sines = sines_all[...].reshape(peers * 8, FREQ_DIM).astype(bf16)
        grad_pre = ((grad_shift + grad_scale) * silu_slope(pre[...])).astype(bf16)
        time_out[...] = time_in[...] - inner_rate * dot(sines, grad_pre, tn)

    def quantize(i):
        slot = lax.rem(i, 2)
        for copy in load(i, slot):
            copy.wait()

        @pl.when(i + 1 < blocks)
        def _():
            for copy in load(i + 1, 1 - slot):
                copy.start()

        for who in range(8):
            for part in range(cols // 128):
                lanes = pl.ds(who * cols + part * 128, 128)
                delta = start_v[slot, :, lanes].astype(jnp.float32) - cur_v[
                    slot, :, lanes
                ].astype(jnp.float32)
                top = jnp.max(jnp.abs(delta), axis=0, keepdims=True)
                scale = (top + epsilon).astype(jnp.bfloat16).astype(jnp.float32)
                level = nearest(delta * (7.0 * TIE_UP / scale))
                level = jnp.clip(level, -7.0, 7.0)
                terms[i, who % 2, who // 2, :, pl.ds(part * 128, 128)] = (
                    level * (scale / 7.0)
                ).astype(jnp.bfloat16)
        step1(i).start()

    def fold1(i):
        step1(i).wait()
        for k in range(4):
            terms[i, core, k] = (
                terms[i, core, k].astype(jnp.float32) + got1[i, k].astype(jnp.float32)
            ).astype(jnp.bfloat16)
        for copy in step2(i):
            copy.start()

    def fold2(i):
        first, second = bits(i)
        for k, copy in enumerate(step2(i)):
            copy.wait()
            at = pair_at(me, first, second, k)
            terms[i, core, at] = (
                terms[i, core, at].astype(jnp.float32) + got2[i, k].astype(jnp.float32)
            ).astype(jnp.bfloat16)
            if k == 0:
                step3(i).start()

    def update(i):
        step3(i).wait()

        @pl.when(i == 0)
        def _():
            for copy in state_loads:
                copy.wait()

        span = pl.ds(pl.multiple_of(i * rows, rows), rows)
        average = (
            terms[i, core, me // 2].astype(jnp.float32) + got3[i].astype(jnp.float32)
        ) / 8.0
        new_momentum = momentum_decay * mom_v[span, :] + average
        new_anchor = anchor_v[span, :] - outer_rate * (average + momentum_decay * new_momentum)
        mom_v[span, :] = new_momentum
        anchor_v[span, :] = new_anchor
        own[i] = new_anchor.astype(jnp.bfloat16)
        back3(i).start()
        back2(i)[0].start()
        back1(i)[0].start()
        keep(i).start()
        pltpu.make_async_copy(anchor_v.at[span, :], anchor_out.at[span, :], store_sem.at[0, i]).start()
        pltpu.make_async_copy(mom_v.at[span, :], mom_out.at[span, :], store_sem.at[1, i]).start()

    def spread2(i):
        back3(i).wait()
        back2(i)[1].start()
        back1(i)[1].start()

    def spread1(i):
        for n, copy in enumerate(back2(i)):
            copy.wait()
            back1(i)[2 + n].start()

    stages = ((9, spread1), (7, spread2), (5, update), (0, quantize), (1, fold1), (3, fold2))
    last = max(lag for lag, _ in stages)

    parts = [(2, inner_open)]
    parts += [(3 + k, lambda k=k: inner_first(peers - 1 - k)) for k in range(peers)]
    at = 5 + peers
    parts += [(at, inner_gather)]
    parts += [(at + q, lambda q=q: inner_sample(q)) for q in range(here)]
    at += here
    parts += [(at - 1, inner_second), (at + 1, inner_close)]
    parts += [(at + 1 + d, lambda d=d: inner_source(d)) for d in range(peers)]
    parts += [(at + 1 + peers, inner_end)]

    def step(i, carry):
        for lag, stage in stages:

            @pl.when(jnp.logical_and(i >= lag, i < blocks + lag))
            def _(stage=stage, lag=lag):
                stage(i - lag)

        for when, part in parts:

            @pl.when(i == when)
            def _(part=part):
                part()

        return carry

    lax.fori_loop(0, max(blocks + last, parts[-1][0] + 1), step, 0)

    def finish(i, carry):
        span = pl.ds(pl.multiple_of(i * rows, rows), rows)
        for copy in back1(i):
            copy.wait()
        keep(i).wait()
        pltpu.make_async_copy(anchor_v.at[span, :], anchor_out.at[span, :], store_sem.at[0, i]).wait()
        pltpu.make_async_copy(mom_v.at[span, :], mom_out.at[span, :], store_sem.at[1, i]).wait()
        return carry

    lax.fori_loop(0, blocks, finish, 0)


def hand_on(arrays):
    pieces = []
    for n, a in enumerate(arrays):
        rows = a.shape[0]
        size = QBLOCK if rows % QBLOCK == 0 else rows
        pieces += [(n, at, size) for at in range(0, rows, size)]

    def kernel(*refs):
        count = len(arrays)
        ins, outs, sem = refs[:count], refs[count : 2 * count], refs[2 * count]

        def move(k):
            n, at, size = pieces[k]
            rows = pl.ds(at, size)
            return pltpu.make_async_copy(ins[n].at[rows], outs[n].at[rows], sem.at[k])

        for k in range(len(pieces)):
            move(k).start()
        for k in range(len(pieces)):
            move(k).wait()

    dma = pltpu.SemaphoreType.DMA
    return pl.pallas_call(
        kernel,
        out_shape=tuple(jax.ShapeDtypeStruct(a.shape, a.dtype) for a in arrays),
        in_specs=[pl.BlockSpec(memory_space=pl.ANY)] * len(arrays),
        out_specs=(pl.BlockSpec(memory_space=pl.ANY),) * len(arrays),
        scratch_shapes=[dma((len(pieces),))],
        compiler_params=pltpu.CompilerParams(vmem_limit_bytes=60 * 1024 * 1024),
        name="hand_on",
    )(*arrays)


def window_by_kernel(
    latents,
    target,
    timesteps,
    patch_weight,
    head_weight,
    modulation,
    time_weight,
    anchor,
    momentum,
    frag_start,
    frag_current,
):
    rows, span = frag_start.shape
    blocks, cols = rows // QBLOCK, anchor.shape[1]
    peers, here = lax.axis_size("fsdp"), timesteps.shape[0]
    width = patch_weight.shape[2]
    group = here * PATCH_DIM
    bf16, f32 = jnp.bfloat16, jnp.float32
    dma = pltpu.SemaphoreType.DMA
    sines = lax.reduce_precision(sinusoid(timesteps), 8, 7)
    sines = jnp.pad(sines, ((0, 8 - here), (0, 0)))
    params = (patch_weight[0], head_weight[0], modulation[0], time_weight[0])
    out = pl.pallas_call(
        lambda *refs: window_kernel(blocks, cols, peers, here, *refs),
        out_shape=tuple(jax.ShapeDtypeStruct(p.shape, f32) for p in params)
        + (
            jax.ShapeDtypeStruct((rows, cols), f32),
            jax.ShapeDtypeStruct((rows, cols), f32),
            jax.ShapeDtypeStruct((rows, span), bf16),
        ),
        in_specs=[pl.BlockSpec(memory_space=pl.ANY)] * 4
        + [pl.BlockSpec(memory_space=pltpu.VMEM)] * 7,
        out_specs=(pl.BlockSpec(memory_space=pltpu.VMEM),) * 4
        + (pl.BlockSpec(memory_space=pl.ANY),) * 3,
        scratch_shapes=[
            pltpu.VMEM((2, QBLOCK, span), bf16),
            pltpu.VMEM((2, QBLOCK, span), bf16),
            pltpu.VMEM((blocks, 2, 4, QBLOCK, cols), bf16),
            pltpu.VMEM((blocks, 4, QBLOCK, cols), bf16),
            pltpu.VMEM((blocks, 2, QBLOCK, cols), bf16),
            pltpu.VMEM((blocks, QBLOCK, cols), bf16),
            pltpu.VMEM((rows, cols), f32),
            pltpu.VMEM((rows, cols), f32),
            pltpu.VMEM((blocks, QBLOCK, cols), bf16),
            dma((2, 2)),
            dma((2,)),
            dma((2, blocks)),
            dma((4, blocks)),
            dma((4, blocks)),
            dma((7, blocks)),
            dma((7, blocks)),
            dma((blocks,)),
            pltpu.VMEM((peers, 8, FREQ_DIM), f32),
            pltpu.VMEM((peers * 8, width), f32),
            pltpu.VMEM((peers * 8, width), f32),
            pltpu.VMEM((peers * 8, width), f32),
            pltpu.VMEM((peers - 1, group + 72, 128), f32),
            pltpu.VMEM((peers, group + 72, 128), f32),
            pltpu.VMEM((group + 72, 128), f32),
            pltpu.VMEM((peers, group + 72, 128), f32),
            pltpu.VMEM((group + 64, 128), f32),
            pltpu.VMEM((64, 128), f32),
            pltpu.VMEM((peers * 8, width), f32),
            pltpu.VMEM((peers * 8, 64), f32),
            dma((3, peers - 1)),
            dma((3, peers - 1)),
        ],
        compiler_params=pltpu.CompilerParams(
            collective_id=0, has_side_effects=True, vmem_limit_bytes=60 * 1024 * 1024
        ),
        cost_estimate=pl.CostEstimate(
            flops=20 * rows * span, bytes_accessed=8 * rows * span, transcendentals=0
        ),
        name="window",
    )(frag_start, frag_current, anchor, momentum, latents.T, target.T, sines, *params)
    out = hand_on(out)
    return tuple(o[None] for o in out[:4]) + tuple(out[4:])


def fragment_by_collectives(anchor, momentum, frag_start, frag_current):
    replica_count = lax.axis_size("replica")
    delta = frag_start.astype(jnp.float32) - frag_current.astype(jnp.float32)
    rows, width = delta.shape
    blocks = delta.reshape(rows // QBLOCK, QBLOCK, width)
    top = jnp.max(jnp.abs(blocks), axis=1, keepdims=True)
    scale = lax.reduce_precision(top + epsilon, 8, 7)
    level = jnp.clip(nearest(blocks * (7.0 * TIE_UP / scale)), -7.0, 7.0)
    terms = (level * (scale / 7.0)).astype(jnp.bfloat16).reshape(rows, width)
    total = lax.psum_scatter(terms, "replica", scatter_dimension=1, tiled=True)
    average = total.astype(jnp.float32) / replica_count
    new_momentum = momentum_decay * momentum + average
    new_anchor = anchor - outer_rate * (average + momentum_decay * new_momentum)
    new_params = lax.all_gather(new_anchor.astype(jnp.bfloat16), "replica", axis=1, tiled=True)
    return new_anchor, new_momentum, new_params


def inner_step(latents, target, timesteps, patch_weight, head_weight, modulation, time_weight):
    fsdp = lax.axis_size("fsdp")
    here = timesteps.shape[0]
    samples = here * fsdp
    width = patch_weight.shape[2]
    full = width * fsdp
    tok_count = latents.shape[0] * fsdp * 1.0
    f32 = jnp.float32

    sines = sinusoid(lax.all_gather(timesteps, "fsdp", tiled=True)).astype(jnp.bfloat16)
    wp = patch_weight[0].astype(jnp.bfloat16).astype(f32)
    wh = head_weight[0].astype(jnp.bfloat16).astype(f32)
    wm = modulation[0].astype(jnp.bfloat16).astype(f32)
    pre_act = jnp.dot(sines, time_weight[0].astype(jnp.bfloat16), preferred_element_type=f32)
    embed = jax.nn.silu(pre_act)
    gain = 1.0 + wm[1] + embed
    shift = wm[0] + embed

    mean_here = jnp.mean(wp, axis=1)
    wp_here = wp - mean_here[:, None]
    gained = wh[None] * gain[:, None, :]
    gram = fdot("if,kf->ik", wp_here, wp_here)
    mix = fdot("sjf,if->sij", gained, wp_here)
    gained_sum = jnp.sum(gained, axis=2)
    offset = fdot("sf,jf->sj", shift, wh)

    def split(a):
        return a.reshape(fsdp, -1, PATCH_DIM)

    def copies(a):
        return jnp.broadcast_to(a.reshape(1, -1, PATCH_DIM), (fsdp, a.size // PATCH_DIM, PATCH_DIM))

    sent = jnp.concatenate(
        [split(mix), split(gained_sum), split(offset), copies(gram), copies(mean_here)], axis=1
    )
    got = lax.all_to_all(sent, "fsdp", 0, 0)
    a, b = here * PATCH_DIM, here * PATCH_DIM + here
    mean_of = got[:, -1]
    mean = jnp.mean(mean_of, axis=0)
    off_mean = mean_of - mean
    gained_sum_of = got[:, a:b]
    mix = jnp.sum(got[:, :a], axis=0).reshape(here, PATCH_DIM, PATCH_DIM) + jnp.sum(
        off_mean[:, None, :, None] * gained_sum_of[:, :, None, :], axis=0
    )
    gained_mean = jnp.sum(gained_sum_of, axis=0) / full
    offset = jnp.sum(got[:, b : b + here], axis=0)
    gram = jnp.sum(got[:, b + here : -1], axis=0) + width * jnp.sum(
        off_mean[:, :, None] * off_mean[:, None, :], axis=0
    )
    gram = gram / full

    lat = latents.astype(f32)
    var = jnp.sum(fdot("ti,ik->tk", lat, gram) * lat, axis=1, keepdims=True)
    inv_std = lax.rsqrt(jnp.maximum(var, 0.0) + epsilon)
    lat = (lat * inv_std).reshape(here, SAMPLE_TOKENS, PATCH_DIM)
    centred = fdot("sti,sij->stj", lat, mix)
    wanted = target.reshape(here, SAMPLE_TOKENS, PATCH_DIM).astype(f32)
    output = centred + offset[:, None, :]
    grad_out = (2.0 * (output - wanted) / tok_count).astype(jnp.bfloat16).astype(f32)
    first = jnp.sum(grad_out * gained_mean[:, None, :], axis=2, keepdims=True)
    second = jnp.sum(grad_out * centred, axis=2, keepdims=True) / full
    cross = fdot("sti,stj->sij", lat, grad_out)
    square = fdot("sti,stk->ik", lat * second, lat)
    lean = jnp.sum(lat * first, axis=(0, 1))
    out_sum = jnp.sum(grad_out, axis=1)

    sent = jnp.concatenate(
        [cross.reshape(-1, PATCH_DIM), out_sum, square, lean[None]], axis=0
    )
    got = lax.all_gather(sent, "fsdp")
    cross = got[:, :a].reshape(samples, PATCH_DIM, PATCH_DIM)
    out_sum = got[:, a:b].reshape(samples, PATCH_DIM)
    square = jnp.sum(got[:, b:-1], axis=0)
    lean = jnp.sum(got[:, -1], axis=0)

    centre = wp - mean[:, None]
    turned = fdot("sij,if->sjf", cross, centre)
    grad_head = jnp.sum(turned * gain[:, None, :], axis=0) + fdot("sj,sf->jf", out_sum, shift)
    grad_scale = jnp.sum(turned * wh[None], axis=1)
    grad_shift = fdot("sj,jf->sf", out_sum, wh)
    grad_patch = (
        fdot("sij,sjf->if", cross, gained)
        - lean[:, None]
        - fdot("ik,kf->if", square, centre)
    )
    grad_mod = jnp.stack([jnp.sum(grad_shift, axis=0), jnp.sum(grad_scale, axis=0)])
    grad_pre = ((grad_shift + grad_scale) * silu_slope(pre_act)).astype(jnp.bfloat16)
    grad_time = lax.dot_general(
        sines, grad_pre, (((0,), (0,)), ((), ())), preferred_element_type=f32
    )
    return (
        patch_weight - inner_rate * grad_patch[None],
        head_weight - inner_rate * grad_head[None],
        modulation - inner_rate * grad_mod[None],
        time_weight - inner_rate * grad_time[None],
    )


def per_device(
    latents,
    target,
    timesteps,
    patch_weight,
    head_weight,
    modulation,
    time_weight,
    anchor,
    momentum,
    frag_start,
    frag_current,
):
    inner = (latents, target, timesteps, patch_weight, head_weight, modulation, time_weight)
    fragment = (anchor, momentum, frag_start, frag_current[0])
    fits = anchor.shape[1] % 128 == 0 and timesteps.shape[0] <= 8
    if lax.axis_size("replica") == 8 and 2 <= lax.axis_size("fsdp") <= 4 and fits:
        return window_by_kernel(*inner, *fragment)
    return inner_step(*inner) + tuple(fragment_by_collectives(*fragment))


def solution(mesh):
    in_specs = (
        P(("replica", "fsdp"), None),
        P(("replica", "fsdp"), None),
        P(("replica", "fsdp")),
        P("replica", None, "fsdp"),
        P("replica", None, "fsdp"),
        P("replica", None, "fsdp"),
        P("replica", None, "fsdp"),
        P("fsdp", "replica"),
        P("fsdp", "replica"),
        P("fsdp", None),
        P("replica", "fsdp", None),
    )
    out_specs = (
        P("replica", None, "fsdp"),
        P("replica", None, "fsdp"),
        P("replica", None, "fsdp"),
        P("replica", None, "fsdp"),
        P("fsdp", "replica"),
        P("fsdp", "replica"),
        P("fsdp", None),
    )
    return jax.shard_map(
        per_device, mesh=mesh, in_specs=in_specs, out_specs=out_specs, check_vma=False
    )
```
